128 devices in a mesh: dp: 32 (over y, x, z_hi), seq: 4 (over z_lo, core).
Axes of the slice: x: 4, y: 4, z: 4 (z_hi: 2, z_lo: 2; z = z_hi * 2 + z_lo), core: 2. Of those that a mesh axis runs over, the one named last changes fastest.
Arguments:
- block_input: bfloat16 [32, 1024, 768], P('dp', 'seq'), may hold values from -6 to 6
- out_grad: bfloat16 [32, 1024, 768], P('dp', 'seq'), may hold values from -6 to 6
- ln1_gain: bfloat16 [768], P('dp'), may hold values from 0.25 to 1.75
- ln1_bias: bfloat16 [768], P('dp'), may hold values from -1.75 to 1.75
- ln2_gain: bfloat16 [768], P('dp'), may hold values from 0.25 to 1.75
- ln2_bias: bfloat16 [768], P('dp'), may hold values from -1.75 to 1.75
- qkv_weight: bfloat16 [768, 2304], P('dp'), may hold values from -0.21875 to 0.21875
- qkv_bias: bfloat16 [2304], P('dp'), may hold values from -3 to 3
- out_weight: bfloat16 [768, 768], P('dp'), may hold values from -0.875 to 0.875
- out_bias: bfloat16 [768], P('dp'), may hold values from -3 to 3
- up_weight: bfloat16 [768, 3072], P('dp'), may hold values from -0.21875 to 0.21875
- up_bias: bfloat16 [3072], P('dp'), may hold values from -3 to 3
- down_weight: bfloat16 [3072, 768], P('dp'), may hold values from -0.109375 to 0.109375
- down_bias: bfloat16 [768], P('dp'), may hold values from -3 to 3
Outputs:
- block_output: bfloat16 [32, 1024, 768], P('dp', 'seq')
- input_grad: bfloat16 [32, 1024, 768], P('dp', 'seq')
- ln1_gain_grad: float32 [768], P('dp')
- ln1_bias_grad: float32 [768], P('dp')
- ln2_gain_grad: float32 [768], P('dp')
- ln2_bias_grad: float32 [768], P('dp')
- qkv_weight_grad: float32 [768, 2304], P('dp')
- qkv_bias_grad: float32 [2304], P('dp')
- out_weight_grad: float32 [768, 768], P('dp')
- out_bias_grad: float32 [768], P('dp')
- up_weight_grad: float32 [768, 3072], P('dp')
- up_bias_grad: float32 [3072], P('dp')
- down_weight_grad: float32 [3072, 768], P('dp')
- down_bias_grad: float32 [768], P('dp')
The draws below stay inside these ranges and needn't reach their ends.
All inputs are finite; a program needn't handle non-finite values.
Results may differ from the reference program's by a relative error of at most 0.025.
Values may be sent and summed in bfloat16 or wider, within the bound.
No kernel may reach another device: no remote copies, remote signals or barrier semaphores. Data moves between devices by JAX's collectives and lax.ppermute only.
A program may use at most 128 MiB of HBM per device.

```python
import jax
import jax.numpy as jnp
from jax import lax

D = 768
H = 12
HD = 64
ROT = 16
FF = 3072
LEN = 1024
BATCH = 32


def spiked(drawn, own_key, source, target, parts, factor):
    def block_of(dim):
        return (jnp.arange(drawn.shape[dim]) // (drawn.shape[dim] // parts)).reshape((-1,) + (1,) * (drawn.ndim - 1 - dim))

    one_side = jax.random.permutation(own_key, parts)[block_of(target)]
    far = (block_of(target) + parts // 2) % parts
    return jnp.where((block_of(source) == one_side) | (block_of(source) == far), factor * drawn, drawn)


def steps_of(stream_key, shape, split, low, high):
    factor_of = 1.0
    for position, shards_of in split:
        steps = jax.random.uniform(jax.random.fold_in(jax.random.fold_in(stream_key, 6), position), (shards_of,), jnp.float32, low / len(split), high / len(split))
        factor_of = factor_of * jnp.repeat(jnp.exp(steps), shape[position] // shards_of).reshape((-1,) + (1,) * (len(shape) - 1 - position))
    return factor_of


def centred(stream_key, dims, scale, bound, pieces=(), held_as=jnp.bfloat16):
    drawn = scale * jax.random.normal(stream_key, dims, jnp.float32)
    if pieces:
        drawn = drawn * steps_of(stream_key, dims, pieces, -0.22, 0.18)
    return jnp.clip(drawn, -bound, bound).astype(held_as)


def gaussian_with(key, shape, scale, limit, cuts, heavy, held_as=jnp.bfloat16):
    array = scale * jax.random.normal(key, shape, jnp.float32)
    if cuts:
        array = array * steps_of(key, shape, cuts, -0.22, 0.18)
    return jnp.clip(spiked(array, jax.random.fold_in(key, 3), *heavy), -limit, limit).astype(held_as)


def setup_inputs(seed: int = 0) -> dict:
    seeds = jax.random.split(jax.random.key(seed), 15)
    block_input = gaussian_with(seeds[0], (BATCH, LEN, D), 1.0, 6.0, ((0, 32), (1, 4)), (0, 2, 32, 2.75))
    out_grad = centred(seeds[1], (BATCH, LEN, D), 1.0, 6.0, ((0, 32), (1, 4)))
    ln1_gain = jnp.clip(1.0 + 0.15 * jax.random.normal(seeds[2], (D,), jnp.float32), 0.25, 1.75).astype(jnp.bfloat16)
    ln1_bias = centred(seeds[3], (D,), 0.3, 1.75, ((0, 32),))
    ln2_gain = jnp.clip(1.0 + 0.15 * jax.random.normal(seeds[4], (D,), jnp.float32), 0.25, 1.75).astype(jnp.bfloat16)
    ln2_bias = centred(seeds[5], (D,), 0.3, 1.75, ((0, 32),))
    qkv_weight = centred(seeds[6], (D, 3 * D), D ** -0.5, 0.21875, ((0, 32),))
    qkv_bias = centred(seeds[7], (3 * D,), 0.5, 3.0, ((0, 32),))
    out_weight = centred(seeds[8], (D, D), (D // 16) ** -0.5, 0.875, ((0, 32),))
    out_bias = centred(seeds[9], (D,), 0.5, 3.0, ((0, 32),))
    up_weight = centred(seeds[10], (D, FF), D ** -0.5, 0.21875, ((0, 32),))
    up_bias = centred(seeds[11], (FF,), 0.5, 3.0, ((0, 32),))
    down_weight = centred(seeds[12], (FF, D), FF ** -0.5, 0.109375, ((0, 32),))
    down_bias = centred(seeds[13], (D,), 0.5, 3.0, ((0, 32),))
    return {"block_input": block_input, "out_grad": out_grad, "ln1_gain": ln1_gain, "ln1_bias": ln1_bias, "ln2_gain": ln2_gain, "ln2_bias": ln2_bias, "qkv_weight": qkv_weight, "qkv_bias": qkv_bias, "out_weight": out_weight, "out_bias": out_bias, "up_weight": up_weight, "up_bias": up_bias, "down_weight": down_weight, "down_bias": down_bias}


@jax.custom_vjp
def low(v):
    return lax.optimization_barrier(v.astype(jnp.bfloat16)).astype(jnp.float32)

@jax.custom_vjp
def low_back(v):
    return v

def low_keep(v):
    return (low(v), None)

def low_pass(kept, grad):
    return (grad,)

def back_keep(v):
    return (v, None)

def back_low(kept, grad):
    return (low(grad),)
low.defvjp(low_keep, low_pass)
low_back.defvjp(back_keep, back_low)

def both_round(values):
    return low(low_back(values))

def layer_norm(values, gain, shift):
    average = lax.optimization_barrier(jnp.mean(values, axis=-1, keepdims=True))
    centered = values - average
    spread = lax.optimization_barrier(jnp.mean(centered * centered, axis=-1, keepdims=True))
    return centered * lax.rsqrt(spread + 1e-05) * gain + shift

def rotary_tables(positions):
    frequency = 10000.0 ** (-2.0 * jnp.arange(ROT // 2, dtype=jnp.float32) / ROT)
    angles = positions[:, None] * frequency[None, :]
    cosine = jnp.cos(angles)
    sine = jnp.sin(angles)
    return (jnp.concatenate([cosine, cosine], -1), jnp.concatenate([sine, sine], -1))

def rotate(vectors, cosine, sine):
    turned_part = vectors[..., :ROT]
    first_half = turned_part[..., :ROT // 2]
    second_half = turned_part[..., ROT // 2:]
    swapped = jnp.concatenate([-second_half, first_half], -1)
    turned_part = turned_part * cosine[:, None, :] + swapped * sine[:, None, :]
    return jnp.concatenate([turned_part, vectors[..., ROT:]], -1)

def attend(query, keys, values):
    block = min(512, LEN)
    count = LEN // block
    scale = HD ** (-0.5)
    highest = lax.Precision.HIGHEST
    query_blocks = query.reshape(count, block, H, HD)
    starts = jnp.arange(count, dtype=jnp.int32) * block

    def one_block(pair):
        query_block, start = pair
        raw = jnp.einsum('qhd,khd->hqk', query_block, keys, precision=highest)
        scores = low_back(raw * scale)
        row_pos = start + jnp.arange(block, dtype=jnp.int32)
        col_pos = jnp.arange(LEN, dtype=jnp.int32)
        allowed = col_pos[None, :] <= row_pos[:, None]
        scores = jnp.where(allowed[None], scores, -1e+30)
        top_score = lax.optimization_barrier(jnp.max(scores, axis=-1, keepdims=True))
        weights = jnp.exp(scores - top_score)
        probs = low(weights / lax.optimization_barrier(jnp.sum(weights, axis=-1, keepdims=True)))
        return jnp.einsum('hqk,khd->qhd', probs, values, precision=highest)
    outputs = lax.map(jax.checkpoint(one_block), (query_blocks, starts))
    return outputs.reshape(LEN, D)

def block_forward(inputs, params):
    gain_one, bias_one, gain_two, bias_two, qkv_w, qkv_b, out_w, out_b, up_w, up_b, down_w, down_b = params
    highest = lax.Precision.HIGHEST
    normed_one = low(layer_norm(inputs, gain_one, bias_one))
    normed_two = low(layer_norm(inputs, gain_two, bias_two))
    mixed = low_back(jnp.dot(normed_one, qkv_w, precision=highest) + qkv_b).reshape(LEN, 3, H, HD)
    positions = jnp.arange(LEN, dtype=jnp.float32)
    cosine, sine = rotary_tables(positions)
    query = both_round(rotate(mixed[:, 0], cosine, sine))
    keys = both_round(rotate(mixed[:, 1], cosine, sine))
    values = both_round(mixed[:, 2])
    context = both_round(attend(query, keys, values))
    attn_out = jnp.dot(context, out_w, precision=highest) + out_b
    upper = low_back(jnp.dot(normed_two, up_w, precision=highest) + up_b)
    active = low(jax.nn.gelu(upper, approximate=False))
    mlp_out = jnp.dot(active, down_w, precision=highest) + down_b
    return inputs + attn_out + mlp_out

def reference(block_input, out_grad, ln1_gain, ln1_bias, ln2_gain, ln2_bias, qkv_weight, qkv_bias, out_weight, out_bias, up_weight, up_bias, down_weight, down_bias):
    params = tuple((p.astype(jnp.float32) for p in (ln1_gain, ln1_bias, ln2_gain, ln2_bias, qkv_weight, qkv_bias, out_weight, out_bias, up_weight, up_bias, down_weight, down_bias)))

    def per_sequence(totals, pair):
        inputs, cotangent = pair
        result, pull = jax.vjp(block_forward, inputs.astype(jnp.float32), params)
        input_part, param_parts = pull(cotangent.astype(jnp.float32))
        totals = tuple((a + b for a, b in zip(totals, param_parts)))
        return (totals, (result.astype(jnp.bfloat16), input_part.astype(jnp.bfloat16)))
    zeros = tuple((jnp.zeros_like(p) for p in params))
    totals, (results, input_parts) = lax.scan(per_sequence, zeros, (block_input, out_grad))
    return (results, input_parts, totals[0], totals[1], totals[2], totals[3], totals[4], totals[5], totals[6], totals[7], totals[8], totals[9], totals[10], totals[11])
```

```python
import jax
import jax.numpy as jnp
from jax import lax
from jax.sharding import PartitionSpec as P

HD = 64
ROT = 16
F32 = jnp.float32
BF = jnp.bfloat16


def swap(value, bits):
    return lax.ppermute(value, "seq", [(s, s ^ bits) for s in range(4)])


def seq_gather(value):
    core = swap(value, 1)
    far = swap(value, 2)
    return [value, core, far, swap(far, 1)]


def seq_reduce(kept, sent):
    pair = kept.astype(F32) + swap(sent, 1).astype(F32)
    return pair[0] + swap(pair[1].astype(BF), 2).astype(F32)


def dp_gather(shard):
    return lax.all_to_all(
        jnp.broadcast_to(shard[None], (32, *shard.shape)), "dp", split_axis=0, concat_axis=0, tiled=True
    )


def dp_reduce(parts):
    got = lax.all_to_all(parts, "dp", split_axis=0, concat_axis=0, tiled=True)
    return jnp.sum(got.astype(F32), axis=0)


def normalize(x):
    average = jnp.mean(x, axis=-1, keepdims=True)
    centered = x - average
    spread = jnp.mean(centered * centered, axis=-1, keepdims=True)
    rstd = lax.rsqrt(spread + 1e-05)
    return centered * rstd, rstd


def rotary_tables(positions):
    frequency = 10000.0 ** (-2.0 * jnp.arange(ROT // 2, dtype=F32) / ROT)
    angles = positions[:, None] * frequency[None, :]
    cosine, sine = jnp.cos(angles), jnp.sin(angles)
    return jnp.concatenate([cosine, cosine], -1), jnp.concatenate([sine, sine], -1)


def rotate(vectors, cosine, sine):
    turned = vectors[..., :ROT]
    swapped = jnp.concatenate([-turned[..., ROT // 2 :], turned[..., : ROT // 2]], -1)
    turned = turned * cosine[:, None, :] + swapped * sine[:, None, :]
    return jnp.concatenate([turned, vectors[..., ROT:]], -1)


def dot(a, b, ca=1, cb=0):
    return lax.dot_general(a, b, (((ca,), (cb,)), ((), ())), preferred_element_type=F32)


def mlp(x, dy, gain, bias, wu, wd, bu):
    xhat, _ = normalize(x.astype(F32))
    h2 = (xhat * gain + bias).astype(BF)
    upper = dot(h2, wu) + bu
    value, pull = jax.vjp(lambda v: jax.nn.gelu(v, approximate=False), upper)
    active = value.astype(BF)
    part = dot(active, wd)
    dupper = pull(dot(dy, wd, 1, 1))[0].astype(BF)
    g_up = dot(h2, dupper, 0, 0)
    g_down = dot(active, dy, 0, 0)
    g_upb = jnp.sum(dupper.astype(F32), axis=0)
    dh2 = dot(dupper, wu, 1, 1)
    return part, g_up, g_down, g_upb, dh2 * gain, jnp.sum(dh2 * xhat, axis=0), jnp.sum(dh2, axis=0)


def attention(x, gain, bias, wqkv, bqkv, position):
    xhat, _ = normalize(x.astype(F32))
    h1 = (xhat * gain + bias).astype(BF)
    mixed = (dot(h1, wqkv) + bqkv).reshape(1024, 3, 3, HD)
    cosine, sine = rotary_tables(position.astype(F32))
    q = rotate(mixed[:, 0], cosine, sine).astype(BF)
    k = rotate(mixed[:, 1], cosine, sine).astype(BF)
    v = mixed[:, 2].astype(BF)
    scores = jnp.einsum("qhd,khd->hqk", q, k, preferred_element_type=F32) * HD**-0.5
    scores = jnp.where((position[None, :] <= position[:, None])[None], scores, -1e30)
    top = jnp.max(scores, axis=-1, keepdims=True)
    weights = jnp.exp(scores - top)
    total = jnp.sum(weights, axis=-1, keepdims=True)
    probs = weights / total
    context = jnp.einsum("hqk,khd->qhd", probs.astype(BF), v, preferred_element_type=F32)
    return h1, (q, k, v, top + jnp.log(total)), context.astype(BF).reshape(1024, 192)


def attention_back(x, h1, saved, dcontext, gain, wqkv, position):
    q, k, v, lse = saved
    xhat, _ = normalize(x.astype(F32))
    scale = HD**-0.5
    dcontext = dcontext.reshape(1024, 3, HD)
    scores = jnp.einsum("qhd,khd->hqk", q, k, preferred_element_type=F32) * scale
    scores = jnp.where((position[None, :] <= position[:, None])[None], scores, -1e30)
    probs = jnp.exp(scores - lse)
    dv = jnp.einsum("hqk,qhd->khd", probs.astype(BF), dcontext, preferred_element_type=F32)
    dprobs = jnp.einsum("qhd,khd->hqk", dcontext, v, preferred_element_type=F32)
    dscores = (probs * (dprobs - jnp.sum(probs * dprobs, axis=-1, keepdims=True))).astype(BF)
    dq = jnp.einsum("hqk,khd->qhd", dscores, k, preferred_element_type=F32) * scale
    dk = jnp.einsum("hqk,qhd->khd", dscores, q, preferred_element_type=F32) * scale
    cosine, sine = rotary_tables(position.astype(F32))
    dq = rotate(dq.astype(BF).astype(F32), cosine, -sine)
    dk = rotate(dk.astype(BF).astype(F32), cosine, -sine)
    dmixed = jnp.stack([dq, dk, dv], axis=1).reshape(1024, 576).astype(BF)
    g_qkv = dot(h1, dmixed, 0, 0)
    g_qkvb = jnp.sum(dmixed.astype(F32), axis=0)
    dh1 = dot(dmixed, wqkv, 1, 1)
    return g_qkv, g_qkvb, dh1 * gain, jnp.sum(dh1 * xhat, axis=0), jnp.sum(dh1, axis=0)


def rows_for(vector):
    return vector.astype(BF).reshape(32, 1, 24)


def per_device(x, dy, g1, b1, g2, b2, wqkv, bqkv, wo, bo, wu, bu, wd, bd):
    s = lax.axis_index("seq")
    x, dy = x[0], dy[0]
    qkv_s = lax.dynamic_index_in_dim(wqkv.reshape(24, 3, 4, 192), s, 2, False).reshape(24, 576)
    up_s = lax.dynamic_index_in_dim(wu.reshape(24, 32, 4, 24), s, 2, False).reshape(24, 768)
    down_s = lax.dynamic_slice_in_dim(wd, s * 24, 24, 0)
    out_s = lax.dynamic_slice_in_dim(wo, s * 192, 192, 1)
    vectors = jnp.stack(
        [g1, b1, g2, b2, bo, bd, lax.dynamic_slice_in_dim(bu, s * 24, 24, 0), *bqkv.reshape(3, 24)]
    )
    vectors = jnp.pad(vectors, ((0, 14), (0, 104)))
    first = dp_gather(jnp.concatenate([up_s, down_s, vectors], axis=1))
    second = dp_gather(jnp.concatenate([qkv_s, out_s], axis=1))
    both = [jnp.concatenate(v, axis=0) for v in zip(*[(b[:256], b[256:]) for b in seq_gather(jnp.concatenate([x, dy]))])]
    xs, dys = both
    position = jnp.concatenate([(s ^ k) * 256 + jnp.arange(256, dtype=jnp.int32) for k in range(4)])

    vec = first[:, :10, 1536:1560]
    rows = jnp.transpose(vec, (1, 0, 2)).reshape(10, 768).astype(F32)
    gain1, bias1, gain2, bias2, bias_o, bias_d, bias_u = [rows[i] for i in range(7)]
    bias_qkv = lax.dynamic_index_in_dim(vec[:, 7:].reshape(3, 4, 192), s, 1, False).reshape(576).astype(F32)
    first = first.reshape(768, 1664)
    part, g_up, g_down, g_upb, dx2, g_gain2, g_bias2 = mlp(
        xs, dys, gain2, bias2, first[:, :768], first[:, 768:1536], bias_u
    )
    sum_first = dp_reduce(
        jnp.concatenate([g_up.astype(BF), g_down.astype(BF)], axis=1).reshape(32, 24, 1536)
    )

    second = second.reshape(768, 768)
    w_qkv = second[:, :576]
    w_out = lax.all_to_all(second[:, 576:].reshape(4, 192, 192), "seq", split_axis=0, concat_axis=0, tiled=True)
    w_out = jnp.transpose(w_out, (1, 0, 2)).reshape(192, 768)
    h1, saved, context = attention(xs, gain1, bias1, w_qkv, bias_qkv, position)
    part = (part + dot(context, w_out)).astype(BF).reshape(2, 2, 256, 768)
    summed = seq_reduce(part[:, 0], part[:, 1])
    block_output = (x.astype(F32) + summed + (bias_o + bias_d)).astype(BF)

    dcontext = dot(dys, w_out, 1, 1).astype(BF)
    g_out = dot(context, dys, 0, 0).astype(BF)
    g_out = lax.all_to_all(
        jnp.transpose(g_out.reshape(192, 4, 192), (1, 0, 2)), "seq", split_axis=0, concat_axis=0, tiled=True
    ).reshape(768, 192)
    g_qkv, g_qkvb, dx1, g_gain1, g_bias1 = attention_back(xs, h1, saved, dcontext, gain1, w_qkv, position)
    dx = (dx1 + dx2).astype(BF).reshape(2, 2, 256, 768)
    dxhat = seq_reduce(dx[:, 0], dx[:, 1])
    xhat, rstd = normalize(x.astype(F32))
    dxhat = dxhat - jnp.mean(dxhat, axis=-1, keepdims=True) - xhat * jnp.mean(dxhat * xhat, axis=-1, keepdims=True)
    input_grad = (dy.astype(F32) + rstd * dxhat).astype(BF)

    g_b = jnp.sum(dy.astype(F32), axis=0)
    g_qkvb = lax.dynamic_update_slice(jnp.zeros((3, 4, 192), F32), g_qkvb.reshape(3, 1, 192), (0, s, 0))
    vec = jnp.concatenate(
        [rows_for(v) for v in (g_gain1, g_bias1, g_gain2, g_bias2, g_b, g_upb)] + [g_qkvb.astype(BF).reshape(32, 3, 24)],
        axis=1,
    )
    vec = jnp.pad(vec, ((0, 0), (0, 15), (0, 104)))
    sum_second = dp_reduce(
        jnp.concatenate([g_qkv.astype(BF).reshape(32, 24, 576), g_out.reshape(32, 24, 192), vec], axis=2)
    )
    every = lax.all_gather(sum_first.astype(BF), "seq", axis=0).astype(F32)
    t_up = jnp.transpose(every[:, :, :768].reshape(4, 24, 32, 24), (1, 2, 0, 3)).reshape(24, 3072)
    t_down = every[:, :, 768:].reshape(96, 768)
    every = lax.all_gather(sum_second.astype(BF), "seq", axis=0).astype(F32)
    t_qkv = jnp.transpose(every[:, :, :576].reshape(4, 24, 3, 192), (1, 2, 0, 3)).reshape(24, 2304)
    t_out = jnp.transpose(every[:, :, 576:768], (1, 0, 2)).reshape(24, 768)
    vec = every[:, :9, 768:792]
    t_vec = jnp.sum(vec, axis=0)
    return (
        block_output[None],
        input_grad[None],
        t_vec[0],
        t_vec[1],
        t_vec[2],
        t_vec[3],
        t_qkv,
        t_vec[6:9].reshape(72),
        t_out,
        t_vec[4],
        t_up,
        vec[:, 5].reshape(96),
        t_down,
        t_vec[4],
    )


def solution(mesh):
    rows, vector, weight = P("dp", "seq", None), P("dp"), P("dp", None)
    params = (vector, vector, vector, vector, weight, vector, weight, vector, weight, vector, weight, vector)
    return jax.shard_map(
        per_device,
        mesh=mesh,
        in_specs=(rows, rows, *params),
        out_specs=(rows, rows, *params),
        check_vma=False,
    )
```

```python
import jax
import jax.numpy as jnp
from jax import lax
from jax.experimental import pallas as pl
from jax.experimental.pallas import tpu as pltpu
from jax.sharding import PartitionSpec as P

HD = 64
ROT = 16
F32 = jnp.float32
BF = jnp.bfloat16


def swap(value, bits):
    return lax.ppermute(value, "seq", [(s, s ^ bits) for s in range(4)])


def seq_gather(value):
    core = swap(value, 1)
    far = swap(value, 2)
    return [value, core, far, swap(far, 1)]


def seq_reduce(kept, sent):
    pair = kept.astype(F32) + swap(sent, 1).astype(F32)
    return pair[0] + swap(pair[1].astype(BF), 2).astype(F32)


def dp_gather(shard):
    return lax.all_to_all(
        jnp.broadcast_to(shard[None], (32, *shard.shape)), "dp", split_axis=0, concat_axis=0, tiled=True
    )


def dp_reduce(parts):
    got = lax.all_to_all(parts, "dp", split_axis=0, concat_axis=0, tiled=True)
    return jnp.sum(got.astype(F32), axis=0)


def normalize(x):
    average = jnp.mean(x, axis=-1, keepdims=True)
    centered = x - average
    spread = jnp.mean(centered * centered, axis=-1, keepdims=True)
    rstd = lax.rsqrt(spread + 1e-05)
    return centered * rstd, rstd


def dot(a, b, ca=1, cb=0):
    return lax.dot_general(a, b, (((ca,), (cb,)), ((), ())), preferred_element_type=F32)


def rotary_tables(position):
    frequency = 10000.0 ** (-2.0 * jnp.arange(ROT // 2, dtype=F32) / ROT)
    angles = position.astype(F32)[:, None] * frequency[None, :]
    cosine, sine = jnp.cos(angles), jnp.sin(angles)
    zero = jnp.zeros_like(sine)
    rest = jnp.zeros((position.shape[0], HD - ROT), F32)
    own = jnp.concatenate([cosine, cosine, rest + 1.0] * 2, -1)
    above = jnp.concatenate([-sine, zero, rest] * 2, -1)
    below = jnp.concatenate([zero, sine, rest] * 2, -1)
    return own, above, below


def turn(block, own, above, below):
    columns = []
    for at in range(0, 384, 128):
        part = block[:, at : at + 128]
        columns.append(part * own + pltpu.roll(part, 120, 1) * above + pltpu.roll(part, 8, 1) * below)
    return jnp.concatenate(columns, -1)


def causal(shape):
    return lax.broadcasted_iota(jnp.int32, shape, 0) <= lax.broadcasted_iota(jnp.int32, shape, 1)


def mlp_kernel(xhat, dy, gain, bias, weights, bu, part, grads, g_upb, dx, g_gain, g_bias, h2_s, act_s, dup_s):
    wu, wd = weights.at[:, 0:768], weights.at[:, 768:1536]
    for ref in (g_upb, g_gain, g_bias):
        ref[...] = jnp.zeros_like(ref)

    @pl.loop(0, 4)
    def _(step):
        rows = pl.ds(pl.multiple_of(step * 256, 256), 256)
        xh = xhat[rows, :]
        h2 = (xh * gain[...] + bias[...]).astype(BF)
        h2_s[rows, :] = h2
        upper = dot(h2, wu[...]) + bu[...]
        phi = 0.5 + 0.5 * lax.erf(upper * 0.7071067811865476)
        active = (upper * phi).astype(BF)
        act_s[rows, :] = active
        slope = phi + upper * (jnp.exp(-0.5 * upper * upper) * 0.3989422804014327)
        dup = (dot(dy[rows, :], wd[...], 1, 1) * slope).astype(BF)
        dup_s[rows, :] = dup
        part[rows, :] = dot(active, wd[...]).astype(BF)
        dh2 = dot(dup, wu[...], 1, 1)
        dx[rows, :] = (dh2 * gain[...]).astype(BF)
        g_upb[...] += jnp.sum(dup.astype(F32), axis=0, keepdims=True)
        g_gain[...] += jnp.sum(dh2 * xh, axis=0, keepdims=True)
        g_bias[...] += jnp.sum(dh2, axis=0, keepdims=True)

    for at in range(0, 768, 256):
        grads[at : at + 256, 0:768] = dot(h2_s[:, at : at + 256], dup_s[...], 0, 0).astype(BF)
        grads[at : at + 256, 768:1536] = dot(act_s[:, at : at + 256], dy[...], 0, 0).astype(BF)


def forward_kernel(
    seq, xhat, dy, gain, bias, weights, bqkv, wo, own, above, below, part, h1, qkv, lse, total, g_out, ctx_s
):
    me = seq[0]

    @pl.loop(0, 4)
    def _(step):
        rows = pl.ds(pl.multiple_of(step * 256, 256), 256)
        place = pl.ds(pl.multiple_of((step ^ me) * 256, 256), 256)
        h = (xhat[rows, :] * gain[...] + bias[...]).astype(BF)
        h1[rows, :] = h
        mixed = dot(h, weights[:, 0:576]) + bqkv[...]
        qkv[place, 0:384] = turn(mixed[:, 0:384], own[rows, :], above[rows, :], below[rows, :]).astype(BF)
        qkv[place, 384:576] = mixed[:, 384:576].astype(BF)

    allowed = causal((256, 256))
    for block in range(4):
        first, keys = block * 256, block * 256 + 256
        for head in range(3):
            at = head * 64
            query = qkv[first:keys, at : at + 64] * 0.125
            scores = dot(qkv[0:keys, 192 + at : 256 + at], query, 1, 1)
            last = jnp.where(allowed, scores[first:], -1e30)
            scores = jnp.concatenate([scores[:first], last], 0) if block else last
            top = jnp.max(scores, axis=0, keepdims=True)
            weight = jnp.exp(scores - top)
            count = jnp.sum(weight, axis=0, keepdims=True)
            lse[head : head + 1, first:keys] = top + jnp.log(count)
            context = dot(qkv[0:keys, 384 + at : 448 + at], weight.astype(BF), 0, 0)
            ctx_s[at : at + 64, :] = context / count
        place = pl.ds(pl.multiple_of((me ^ block) * 256, 256), 256)
        context = ctx_s[...].T.astype(BF)
        total[place, :] = context
        part_rows = part[place, :].astype(F32) + dot(context, wo[...])
        part[place, :] = part_rows.astype(BF)
    g_out[...] = dot(total[...], dy[...], 0, 0).astype(BF)


def backward_kernel(
    seq, xhat, dy, gain, weights, wo, own, above, below, h1, qkv, lse, dx2,
    g_qkv, g_qkvb, dx, g_gain, g_bias, do_s, dq_s, dk_s, dv_s, dm_s,
):
    me = seq[0]
    for ref in (g_qkvb, g_gain, g_bias):
        ref[...] = jnp.zeros_like(ref)

    @pl.loop(0, 4)
    def _(step):
        rows = pl.ds(pl.multiple_of(step * 256, 256), 256)
        place = pl.ds(pl.multiple_of((step ^ me) * 256, 256), 256)
        do_s[place, :] = dot(dy[rows, :], wo[...], 1, 1).astype(BF)

    allowed = causal((256, 256))
    for block in reversed(range(4)):
        first, keys = block * 256, block * 256 + 256
        for head in range(3):
            at = head * 64
            query = qkv[first:keys, at : at + 64] * 0.125
            key = qkv[0:keys, 192 + at : 256 + at]
            dcontext = do_s[first:keys, at : at + 64]
            scores = dot(key, query, 1, 1)
            last = jnp.where(allowed, scores[first:], -1e30)
            scores = jnp.concatenate([scores[:first], last], 0) if block else last
            probs = jnp.exp(scores - lse[head : head + 1, first:keys])
            dprobs = dot(qkv[0:keys, 384 + at : 448 + at], dcontext, 1, 1)
            delta = jnp.sum(probs * dprobs, axis=0, keepdims=True)
            dscores = (probs * (dprobs - delta)).astype(BF)
            dv = dot(probs.astype(BF), dcontext)
            dk = dot(dscores, query)
            if block == 3:
                dv_s[:, at : at + 64] = dv
                dk_s[:, at : at + 64] = dk
            else:
                dv_s[0:keys, at : at + 64] += dv
                dk_s[0:keys, at : at + 64] += dk
            dq_s[at : at + 64, first:keys] = dot(key, dscores, 0, 0) * 0.125

    for block in range(4):
        first, keys = block * 256, block * 256 + 256
        place = pl.ds(pl.multiple_of((me ^ block) * 256, 256), 256)
        both = jnp.concatenate([dq_s[:, first:keys].T, dk_s[first:keys, :]], -1)
        both = both.astype(BF).astype(F32)
        both = turn(both, own[place, :], -above[place, :], -below[place, :])
        dm_s[place, 0:384] = both.astype(BF)
        dm_s[place, 384:576] = dv_s[first:keys, :].astype(BF)

    for at in range(0, 768, 256):
        g_qkv[at : at + 256, :] = dot(h1[:, at : at + 256], dm_s[...], 0, 0).astype(BF)

    @pl.loop(0, 4)
    def _(step):
        rows = pl.ds(pl.multiple_of(step * 256, 256), 256)
        dmixed = dm_s[rows, :]
        dh1 = dot(dmixed, weights[:, 0:576], 1, 1)
        dx[rows, :] = (dh1 * gain[...] + dx2[rows, :].astype(F32)).astype(BF)
        g_qkvb[...] += jnp.sum(dmixed.astype(F32), axis=0, keepdims=True)
        g_gain[...] += jnp.sum(dh1 * xhat[rows, :], axis=0, keepdims=True)
        g_bias[...] += jnp.sum(dh1, axis=0, keepdims=True)


def whole(shape):
    return pl.BlockSpec(shape, lambda i: (0, 0))


def call(kernel, name, flops, args, specs, outs, scratch, aliases={}):
    shapes = [jax.ShapeDtypeStruct(shape, dtype) for shape, dtype in outs]
    moved = sum(a.size * a.dtype.itemsize for a in args) + sum(a.size * a.dtype.itemsize for a in shapes)
    return pl.pallas_call(
        kernel,
        name=name,
        grid=(1,),
        in_specs=[whole(a.shape) if spec is None else spec for a, spec in zip(args, specs)],
        out_specs=[whole(shape.shape) for shape in shapes],
        out_shape=shapes,
        scratch_shapes=[pltpu.VMEM(shape, dtype) for shape, dtype in scratch],
        input_output_aliases=aliases,
        cost_estimate=pl.CostEstimate(flops=flops, bytes_accessed=moved, transcendentals=0),
        compiler_params=pltpu.CompilerParams(vmem_limit_bytes=56 * 2**20),
    )(*args)


def rows_for(vector):
    return vector.astype(BF).reshape(32, 1, 24)


def per_device(x, dy, g1, b1, g2, b2, wqkv, bqkv, wo, bo, wu, bu, wd, bd):
    s = lax.axis_index("seq")
    x, dy = x[0], dy[0]
    qkv_s = lax.dynamic_index_in_dim(wqkv.reshape(24, 3, 4, 192), s, 2, False).reshape(24, 576)
    up_s = lax.dynamic_index_in_dim(wu.reshape(24, 32, 4, 24), s, 2, False).reshape(24, 768)
    down_s = lax.dynamic_slice_in_dim(wd, s * 24, 24, 0)
    out_s = lax.dynamic_slice_in_dim(wo, s * 192, 192, 1)
    vectors = jnp.stack(
        [g1, b1, g2, b2, bo, bd, lax.dynamic_slice_in_dim(bu, s * 24, 24, 0), *bqkv.reshape(3, 24)]
    )
    vectors = jnp.pad(vectors, ((0, 14), (0, 104)))
    gathered = dp_gather(jnp.concatenate([up_s, down_s, qkv_s, out_s, vectors], axis=1))
    blocks = seq_gather(jnp.concatenate([x, dy]))
    xs = jnp.concatenate([b[:256] for b in blocks])
    dys = jnp.concatenate([b[256:] for b in blocks])
    xhat, rstd = normalize(xs.astype(F32))
    position = jnp.concatenate([(s ^ k) * 256 + jnp.arange(256, dtype=jnp.int32) for k in range(4)])
    tables = rotary_tables(position)
    me = s.astype(jnp.int32).reshape(1)
    scalar = pl.BlockSpec(memory_space=pltpu.SMEM)

    vec = gathered[:, :10, 2304:2328]
    rows = jnp.transpose(vec, (1, 0, 2)).reshape(10, 1, 768).astype(F32)
    gain1, bias1, gain2, bias2, bias_o, bias_d, bias_u = [rows[i] for i in range(7)]
    bias_qkv = lax.dynamic_index_in_dim(vec[:, 7:].reshape(3, 4, 192), s, 1, False).reshape(1, 576).astype(F32)
    weights = gathered.reshape(768, 2432)
    w_out = lax.all_to_all(
        weights[:, 2112:2304].reshape(4, 192, 192), "seq", split_axis=0, concat_axis=0, tiled=True
    )
    w_out = jnp.transpose(w_out, (1, 0, 2)).reshape(192, 768)

    wide, row, tall = (1024, 768), (1, 768), [(1024, 768), BF]
    part, grads, g_upb, dx2, g_gain2, g_bias2 = call(
        mlp_kernel,
        "mlp",
        7_300_000_000,
        (xhat, dys, gain2, bias2, weights, bias_u),
        (None, None, None, None, whole((768, 1536)), None),
        [(wide, BF), ((768, 1536), BF), (row, F32), (wide, BF), (row, F32), (row, F32)],
        [tall, tall, tall],
    )
    sum_first = dp_reduce(grads.reshape(32, 24, 1536))
    w_spec = pl.BlockSpec((768, 768), lambda i: (0, 2))

    def forward(seq, xh, d, gain, bias, w, bq, w_o, own, above, below, before, part, *rest):
        part[...] = before[...]
        forward_kernel(seq, xh, d, gain, bias, w, bq, w_o, own, above, below, part, *rest)

    part, h1, qkv, lse, context, g_out = call(
        forward,
        "attention_forward",
        3_000_000_000,
        (me, xhat, dys, gain1, bias1, weights, bias_qkv, w_out, *tables, part),
        (scalar, None, None, None, None, w_spec, None, None, None, None, None, None),
        [(wide, BF), (wide, BF), ((1024, 576), BF), ((8, 1024), F32), ((1024, 192), BF), ((192, 768), BF)],
        [((192, 256), F32)],
    )
    part = part.reshape(2, 2, 256, 768)
    summed = seq_reduce(part[:, 0], part[:, 1])
    block_output = (x.astype(F32) + summed + (bias_o + bias_d)).astype(BF)
    g_out = lax.all_to_all(
        jnp.transpose(g_out.reshape(192, 4, 192), (1, 0, 2)), "seq", split_axis=0, concat_axis=0, tiled=True
    ).reshape(768, 192)

    g_qkv, g_qkvb, dx, g_gain1, g_bias1 = call(
        backward_kernel,
        "attention_backward",
        5_000_000_000,
        (me, xhat, dys, gain1, weights, w_out, *tables, h1, qkv, lse, dx2),
        (scalar, None, None, None, w_spec, None, None, None, None, None, None, None, None),
        [((768, 576), BF), ((1, 576), F32), (wide, BF), (row, F32), (row, F32)],
        [((1024, 192), BF), ((192, 1024), F32), ((1024, 192), F32), ((1024, 192), F32), ((1024, 576), BF)],
    )
    dx = dx.reshape(2, 2, 256, 768)
    dxhat = seq_reduce(dx[:, 0], dx[:, 1])
    xhat, rstd = xhat[:256], rstd[:256]
    dxhat = dxhat - jnp.mean(dxhat, axis=-1, keepdims=True) - xhat * jnp.mean(dxhat * xhat, axis=-1, keepdims=True)
    input_grad = (dy.astype(F32) + rstd * dxhat).astype(BF)

    g_b = jnp.sum(dy.astype(F32), axis=0)
    g_qkvb = lax.dynamic_update_slice(jnp.zeros((3, 4, 192), F32), g_qkvb.reshape(3, 1, 192), (0, s, 0))
    vec = jnp.concatenate(
        [rows_for(v) for v in (g_gain1, g_bias1, g_gain2, g_bias2, g_b, g_upb)] + [g_qkvb.astype(BF).reshape(32, 3, 24)],
        axis=1,
    )
    vec = jnp.pad(vec, ((0, 0), (0, 15), (0, 104)))
    sum_second = dp_reduce(
        jnp.concatenate([g_qkv.astype(BF).reshape(32, 24, 576), g_out.reshape(32, 24, 192), vec], axis=2)
    )
    every = lax.all_gather(sum_first.astype(BF), "seq", axis=0).astype(F32)
    t_up = jnp.transpose(every[:, :, :768].reshape(4, 24, 32, 24), (1, 2, 0, 3)).reshape(24, 3072)
    t_down = every[:, :, 768:].reshape(96, 768)
    every = lax.all_gather(sum_second.astype(BF), "seq", axis=0).astype(F32)
    t_qkv = jnp.transpose(every[:, :, :576].reshape(4, 24, 3, 192), (1, 2, 0, 3)).reshape(24, 2304)
    t_out = jnp.transpose(every[:, :, 576:768], (1, 0, 2)).reshape(24, 768)
    vec = every[:, :9, 768:792]
    t_vec = jnp.sum(vec, axis=0)
    return (
        block_output[None],
        input_grad[None],
        t_vec[0],
        t_vec[1],
        t_vec[2],
        t_vec[3],
        t_qkv,
        t_vec[6:9].reshape(72),
        t_out,
        t_vec[4],
        t_up,
        vec[:, 5].reshape(96),
        t_down,
        t_vec[4],
    )


def solution(mesh):
    rows, vector, weight = P("dp", "seq", None), P("dp"), P("dp", None)
    params = (vector, vector, vector, vector, weight, vector, weight, vector, weight, vector, weight, vector)
    return jax.shard_map(
        per_device,
        mesh=mesh,
        in_specs=(rows, rows, *params),
        out_specs=(rows, rows, *params),
        check_vma=False,
    )
```

```python
import jax
import jax.numpy as jnp
from jax import lax
from jax.experimental import pallas as pl
from jax.experimental.pallas import tpu as pltpu
from jax.sharding import PartitionSpec as P

HD = 64
ROT = 16
F32 = jnp.float32
BF = jnp.bfloat16


def swap(value, bits):
    return lax.ppermute(value, "seq", [(s, s ^ bits) for s in range(4)])


def seq_gather(value):
    far = swap(value, 2)
    return [value, swap(value, 1), far, swap(far, 1)]


def seq_reduce(kept, sent):
    pair = kept.astype(F32) + swap(sent, 1).astype(F32)
    return pair[0] + swap(pair[1].astype(BF), 2).astype(F32)


def dp_groups():
    return [[2 * p + z for p in range(16)] for z in range(2)]


def plane_exchange(parts):
    return lax.all_to_all(
        parts.reshape(16, 48, -1), "dp", split_axis=0, concat_axis=0, tiled=True, axis_index_groups=dp_groups()
    )


def dp_shift(value, along_y, along_x):
    pairs = []
    for d in range(32):
        y, x, z = d // 8, d // 2 % 4, d % 2
        pairs.append((d, ((y + along_y) % 4 * 4 + (x + along_x) % 4) * 2 + z))
    return lax.ppermute(value, "dp", pairs)


def across_pair(value):
    return lax.ppermute(value, "dp", [(d, d ^ 1) for d in range(32)])


SOURCES = (0, -1, 1, 2)


def dp_gather(shard, cut):
    other = across_pair(shard)
    low = lax.axis_index("dp") % 2 == 0
    pair = jnp.concatenate([jnp.where(low, shard, other), jnp.where(low, other, shard)], axis=0)
    left, right = [pair[:, :cut]], [pair[:, cut:]]
    for step in SOURCES[1:]:
        left.append(dp_shift(left[0], 0, -step))
        right.append(dp_shift(right[0], -step, 0))
    left, right = [jnp.concatenate(left)], [jnp.concatenate(right)]
    for step in SOURCES[1:]:
        left.append(dp_shift(left[0], -step, 0))
        right.append(dp_shift(right[0], 0, -step))
    return left, right


def plane_sum(parts):
    return jnp.sum(parts.astype(F32), axis=0)


def pair_sum(total):
    half = lax.axis_index("dp") % 2
    kept = lax.dynamic_slice_in_dim(total, half * 24, 24, 0)
    sent = lax.dynamic_slice_in_dim(total, (1 - half) * 24, 24, 0).astype(BF)
    return (kept + across_pair(sent).astype(F32)).astype(BF)


def normalize(x):
    average = jnp.mean(x, axis=-1, keepdims=True)
    centered = x - average
    spread = jnp.mean(centered * centered, axis=-1, keepdims=True)
    rstd = lax.rsqrt(spread + 1e-05)
    return centered * rstd, rstd


def dot(a, b, ca=1, cb=0):
    return lax.dot_general(a, b, (((ca,), (cb,)), ((), ())), preferred_element_type=F32)


def rotary_tables(position):
    frequency = 10000.0 ** (-2.0 * jnp.arange(ROT // 2, dtype=F32) / ROT)
    angles = position.astype(F32)[:, None] * frequency[None, :]
    cosine, sine = jnp.cos(angles), jnp.sin(angles)
    zero = jnp.zeros_like(sine)
    rest = jnp.zeros((position.shape[0], HD - ROT), F32)
    own = jnp.concatenate([cosine, cosine, rest + 1.0] * 2, -1)
    above = jnp.concatenate([-sine, zero, rest] * 2, -1)
    below = jnp.concatenate([zero, sine, rest] * 2, -1)
    return own, above, below


def turn(block, own, above, below):
    columns = []
    for at in range(0, 384, 128):
        part = block[:, at : at + 128]
        columns.append(part * own + pltpu.roll(part, 120, 1) * above + pltpu.roll(part, 8, 1) * below)
    return jnp.concatenate(columns, -1)


def causal(shape):
    return lax.broadcasted_iota(jnp.int32, shape, 0) <= lax.broadcasted_iota(jnp.int32, shape, 1)


def by24(index):
    return jnp.floor((index.astype(F32) + 0.5) * (1.0 / 24.0)).astype(jnp.int32)


def lane(n):
    return lax.broadcasted_iota(jnp.int32, (1, n), 1)


def sublane(n):
    return lax.broadcasted_iota(jnp.int32, (n, 1), 0)


def one_hot(rows, columns):
    return jnp.where(rows == columns, 1.0, 0.0).astype(BF)


def bias_places(me):
    column = sublane(576)
    column = column + 576 * ((column >= 192).astype(jnp.int32) + (column >= 384).astype(jnp.int32)) + 192 * me
    target = lane(768)
    target = target + 48 * by24(target)
    return [one_hot(column, target + 24 * third) for third in range(3)]


def pack_kernel(seq, wqkv, wo, wu, wd, vec, out):
    me = seq[0]

    def chosen(pieces):
        result = pieces[0]
        for at in range(1, 4):
            result = jnp.where(me == at, pieces[at], result)
        return result

    target = lane(384)
    target = target + 72 * by24(target) + 24 * me
    pick = one_hot(sublane(1536), target)
    up = [dot(wu[:, 0:1536], pick), dot(wu[:, 1536:3072], pick)]
    rows = wd[...].astype(F32)
    down = chosen([rows[24 * q : 24 * q + 24] for q in range(4)])
    columns = wqkv[...].astype(F32)
    qkv = [chosen([columns[:, k + 192 * q : k + 192 * q + 192] for q in range(4)]) for k in (0, 768, 1536)]
    columns = wo[...].astype(F32)
    outs = chosen([columns[:, 192 * q : 192 * q + 192] for q in range(4)])
    vectors = vec[...].T[0:24, 0:64]
    out[...] = jnp.concatenate([*up, *qkv[:2], down, qkv[2], outs, vectors], axis=1).astype(BF)


def mlp_kernel(
    place, xhat, dy, left_0, left_1, left_2, left_3, right_0, right_1, right_2, right_3,
    part, grads, sums, dx, wqkv, w_out, vectors, h2_s, act_s, dup_s, wu, wd, wo_s, vec_s,
):
    me, y, x = place[0], place[1], place[2]
    for outer, (left, right) in enumerate(
        ((left_0, right_0), (left_1, right_1), (left_2, right_2), (left_3, right_3))
    ):
        for inner in range(4):
            one = lax.rem(y + (SOURCES[outer] + 4), 4) * 4 + lax.rem(x + (SOURCES[inner] + 4), 4)
            rows = pl.ds(pl.multiple_of(one * 48, 48), 48)
            piece = left[inner * 48 : inner * 48 + 48, :]
            wu[rows, :] = piece[:, 0:768]
            wqkv[rows, 0:384] = piece[:, 768:1152]
            one = lax.rem(y + (SOURCES[inner] + 4), 4) * 4 + lax.rem(x + (SOURCES[outer] + 4), 4)
            rows = pl.ds(pl.multiple_of(one * 48, 48), 48)
            piece = right[inner * 48 : inner * 48 + 48, :]
            wd[rows, :] = piece[:, 0:768]
            wqkv[rows, 384:576] = piece[:, 768:960]
            wo_s[rows, :] = piece[:, 960:1152]
            vec_s[rows, 0:64] = piece[:, 1152:1216].astype(F32)
    for at in range(4):
        w_out[at] = wo_s[pl.ds(pl.multiple_of((me ^ at) * 192, 192), 192), :]
    vectors[...] = vec_s[...].T[0:16]
    sums[...] = jnp.zeros_like(sums)

    @pl.loop(0, 4)
    def _(step):
        rows = pl.ds(pl.multiple_of(step * 256, 256), 256)
        xh = xhat[rows, :]
        gain = vectors[2:3, :]
        h2 = (xh * gain + vectors[3:4, :]).astype(BF)
        h2_s[rows, :] = h2
        upper = dot(h2, wu[...]) + vectors[6:7, :]
        phi = 0.5 + 0.5 * lax.erf(upper * 0.7071067811865476)
        active = (upper * phi).astype(BF)
        act_s[rows, :] = active
        slope = phi + upper * (jnp.exp(-0.5 * upper * upper) * 0.3989422804014327)
        dup = (dot(dy[rows, :], wd[...], 1, 1) * slope).astype(BF)
        dup_s[rows, :] = dup
        part[rows, :] = dot(active, wd[...]).astype(BF)
        dh2 = dot(dup, wu[...], 1, 1)
        dx[rows, :] = (dh2 * gain).astype(BF)
        sums[0:1, :] += jnp.sum(dh2 * xh, axis=0, keepdims=True)
        sums[1:2, :] += jnp.sum(dh2, axis=0, keepdims=True)
        sums[2:3, :] += jnp.sum(dup.astype(F32), axis=0, keepdims=True)

    for at in range(0, 768, 256):
        grads[at : at + 256, 0:768] = dot(h2_s[:, at : at + 256], dup_s[...], 0, 0).astype(BF)
        grads[at : at + 256, 768:1536] = dot(act_s[:, at : at + 256], dy[...], 0, 0).astype(BF)


def forward_kernel(
    seq, xhat, dy, weights, vec_s, own, above, below, h1, qkv, lse, total, g_out, ctx_s
):
    me = seq[0]
    bias_qkv = jnp.zeros((1, 576), F32)
    for third, place in enumerate(bias_places(me)):
        bias_qkv += dot(vec_s[7 + third : 8 + third, :].astype(BF), place, 1, 1)

    @pl.loop(0, 4)
    def _(step):
        rows = pl.ds(pl.multiple_of(step * 256, 256), 256)
        place = pl.ds(pl.multiple_of((step ^ me) * 256, 256), 256)
        h = (xhat[rows, :] * vec_s[0:1, :] + vec_s[1:2, :]).astype(BF)
        h1[rows, :] = h
        mixed = dot(h, weights[...]) + bias_qkv
        qkv[place, 0:384] = turn(mixed[:, 0:384], own[rows, :], above[rows, :], below[rows, :]).astype(BF)
        qkv[place, 384:576] = mixed[:, 384:576].astype(BF)

    allowed = causal((256, 256))
    for block in range(4):
        first, keys = block * 256, block * 256 + 256
        for head in range(3):
            at = head * 64
            query = qkv[first:keys, at : at + 64] * 0.125
            scores = dot(qkv[0:keys, 192 + at : 256 + at], query, 1, 1)
            last = jnp.where(allowed, scores[first:], -1e30)
            scores = jnp.concatenate([scores[:first], last], 0) if block else last
            top = jnp.max(scores, axis=0, keepdims=True)
            weight = jnp.exp(scores - top)
            count = jnp.sum(weight, axis=0, keepdims=True)
            lse[head : head + 1, first:keys] = top + jnp.log(count)
            context = dot(qkv[0:keys, 384 + at : 448 + at], weight.astype(BF), 0, 0)
            ctx_s[at : at + 64, :] = context / count
        place = pl.ds(pl.multiple_of((me ^ block) * 256, 256), 256)
        total[place, :] = ctx_s[...].T.astype(BF)
    rows = dot(total[...], dy[...], 0, 0)
    for column in range(4):
        g_out[column ^ me] = rows[:, 192 * column : 192 * column + 192].astype(BF)


def backward_kernel(
    seq, xhat, dy, weights, vec_s, wo_0, wo_1, wo_2, wo_3, own, above, below, h1, qkv, lse, context, before, dx2, sums,
    grads, part, dx, do_s, dq_s, dk_s, dv_s, dm_s, sum_s, pieces, wo,
):
    me = seq[0]
    sum_s[...] = jnp.zeros_like(sum_s)
    for at, piece in enumerate((wo_0, wo_1, wo_2, wo_3)):
        pieces[at] = piece[...]
    for at in range(4):
        wo[:, 192 * at : 192 * at + 192] = pieces[at ^ me]
    bias_out = jnp.where(me == 0, vec_s[4:5, :] + vec_s[5:6, :], 0.0)

    @pl.loop(0, 4)
    def _(step):
        rows = pl.ds(pl.multiple_of(step * 256, 256), 256)
        place = pl.ds(pl.multiple_of((step ^ me) * 256, 256), 256)
        do_s[place, :] = dot(dy[rows, :], wo[...], 1, 1).astype(BF)
        part[rows, :] = (before[rows, :].astype(F32) + dot(context[rows, :], wo[...]) + bias_out).astype(BF)

    allowed = causal((256, 256))
    for block in reversed(range(4)):
        first, keys = block * 256, block * 256 + 256
        for head in range(3):
            at = head * 64
            query = qkv[first:keys, at : at + 64] * 0.125
            key = qkv[0:keys, 192 + at : 256 + at]
            dcontext = do_s[first:keys, at : at + 64]
            scores = dot(key, query, 1, 1)
            last = jnp.where(allowed, scores[first:], -1e30)
            scores = jnp.concatenate([scores[:first], last], 0) if block else last
            probs = jnp.exp(scores - lse[head : head + 1, first:keys])
            dprobs = dot(qkv[0:keys, 384 + at : 448 + at], dcontext, 1, 1)
            delta = jnp.sum(probs * dprobs, axis=0, keepdims=True)
            dscores = (probs * (dprobs - delta)).astype(BF)
            dv = dot(probs.astype(BF), dcontext)
            dk = dot(dscores, query)
            if block == 3:
                dv_s[:, at : at + 64] = dv
                dk_s[:, at : at + 64] = dk
            else:
                dv_s[0:keys, at : at + 64] += dv
                dk_s[0:keys, at : at + 64] += dk
            dq_s[at : at + 64, first:keys] = dot(key, dscores, 0, 0) * 0.125

    for block in range(4):
        first, keys = block * 256, block * 256 + 256
        place = pl.ds(pl.multiple_of((me ^ block) * 256, 256), 256)
        both = jnp.concatenate([dq_s[:, first:keys].T, dk_s[first:keys, :]], -1)
        both = both.astype(BF).astype(F32)
        both = turn(both, own[place, :], -above[place, :], -below[place, :])
        dm_s[place, 0:384] = both.astype(BF)
        dm_s[place, 384:576] = dv_s[first:keys, :].astype(BF)

    bias_qkv = jnp.zeros((1, 576), F32)
    for step in range(4):
        rows = slice(step * 256, step * 256 + 256)
        dmixed = dm_s[rows, :]
        dh1 = dot(dmixed, weights[...], 1, 1)
        dx[rows, :] = (dh1 * vec_s[0:1, :] + dx2[rows, :].astype(F32)).astype(BF)
        bias_qkv += jnp.sum(dmixed.astype(F32), axis=0, keepdims=True)
        sum_s[0:1, :] += jnp.sum(dh1 * xhat[rows, :], axis=0, keepdims=True)
        sum_s[1:2, :] += jnp.sum(dh1, axis=0, keepdims=True)
    sum_s[2:4, :] = sums[0:2, :]
    sum_s[4:5, :] = jnp.sum(dy[0:256, :].astype(F32), axis=0, keepdims=True)
    sum_s[5:6, :] = sums[2:3, :]
    for third, place in enumerate(bias_places(me)):
        sum_s[6 + third : 7 + third, :] = dot(bias_qkv.astype(BF), place)
    columns = sum_s[...].T[:, 0:64]
    for at in range(0, 768, 256):
        chunk = dot(h1[:, at : at + 256], dm_s[...], 0, 0)
        grads[at : at + 256, :] = jnp.concatenate([chunk, columns[at : at + 256]], -1).astype(BF)


def first_kernel(every, up, down):
    row = sublane(384)
    group = jnp.floor((row.astype(F32) + 0.5) * (1.0 / 96.0)).astype(jnp.int32)
    inner = row - 96 * group
    pick = one_hot(inner + 72 * by24(inner) + 24 * group, lane(384))
    parts = [every[at].astype(F32) for at in range(4)]
    for at in range(8):
        columns = jnp.concatenate([p[:, 96 * at : 96 * at + 96] for p in parts], -1).astype(BF)
        up[:, 384 * at : 384 * at + 384] = dot(columns, pick)
    down[...] = jnp.concatenate([p[:, 768:1536] for p in parts], 0)


def second_kernel(every, qkv, out, *small):
    parts = [every[at].astype(F32) for at in range(4)]
    for kind in range(3):
        qkv[:, 768 * kind : 768 * kind + 768] = jnp.concatenate(
            [p[:, 192 * kind : 192 * kind + 192] for p in parts], -1
        )
    out[...] = jnp.concatenate([p[:, 640:832] for p in parts], -1)
    pad = jnp.zeros((104, 64), F32)
    rows = [jnp.concatenate([p[:, 576:640], pad], 0).T for p in parts]
    total = rows[0] + rows[1] + rows[2] + rows[3]
    for at, ref in enumerate(small[:5]):
        ref[...] = total[at, 0:24]
    small[5][...] = jnp.concatenate([total[at : at + 1, 0:24] for at in (6, 7, 8)], -1)[0]
    small[6][...] = jnp.concatenate([r[5:6, 0:24] for r in rows], -1)[0]


def whole(shape):
    return pl.BlockSpec(shape, lambda i: (0,) * len(shape))


def call(kernel, name, args, specs, outs, scratch=()):
    shapes = [jax.ShapeDtypeStruct(shape, dtype) for shape, dtype in outs]
    return pl.pallas_call(
        kernel,
        name=name,
        grid=(1,),
        in_specs=[whole(a.shape) if spec is None else spec for a, spec in zip(args, specs)],
        out_specs=[whole(shape.shape) for shape in shapes],
        out_shape=shapes,
        scratch_shapes=[pltpu.VMEM(shape, dtype) for shape, dtype in scratch],
        cost_estimate=pl.CostEstimate(flops=1_000_000, bytes_accessed=100_000, transcendentals=0),
        compiler_params=pltpu.CompilerParams(vmem_limit_bytes=56 * 2**20),
    )(*args)


def per_device(x, dy, g1, b1, g2, b2, wqkv, bqkv, wo, bo, wu, bu, wd, bd):
    s = lax.axis_index("seq")
    me = s.astype(jnp.int32).reshape(1)
    scalar = pl.BlockSpec(memory_space=pltpu.SMEM)
    x, dy = x[0], dy[0]
    x_blocks = seq_gather(x)
    dy_blocks = seq_gather(dy)

    vectors = [g1, b1, g2, b2, bo, bd, lax.dynamic_slice_in_dim(bu, s * 24, 24, 0), *bqkv.reshape(3, 24)]
    vectors = jnp.pad(jnp.stack(vectors).astype(F32), ((0, 118), (0, 104)))
    (packed,) = call(
        pack_kernel, "pack", (me, wqkv, wo, wu, wd, vectors), (scalar, *[None] * 5), [((24, 2368), BF)]
    )
    left, right = dp_gather(packed, 1152)

    xs, dys = jnp.concatenate(x_blocks), jnp.concatenate(dy_blocks)
    xhat, rstd = normalize(xs.astype(F32))
    position = jnp.concatenate([(s ^ k) * 256 + jnp.arange(256, dtype=jnp.int32) for k in range(4)])
    xhat, *tables = lax.optimization_barrier((xhat, *rotary_tables(position)))

    wide, tall, lines = (1024, 768), [(1024, 768), BF], ((16, 768), F32)
    d = lax.axis_index("dp").astype(jnp.int32)
    place = jnp.stack([s.astype(jnp.int32), d // 8, d // 2 % 4])
    part, grads, sums, dx2, w_qkv, w_out, vectors = call(
        mlp_kernel,
        "mlp",
        (place, xhat, dys, *left, *right),
        (scalar, *[None] * 10),
        [
            (wide, BF),
            ((768, 1536), BF),
            ((8, 768), F32),
            (wide, BF),
            ((768, 576), BF),
            ((4, 192, 192), BF),
            lines,
        ],
        [tall, tall, tall, ((768, 768), BF), ((768, 768), BF), ((768, 192), BF), ((768, 128), F32)],
    )
    plane_first = plane_exchange(grads)
    w_out = [w_out[0]] + [swap(w_out[k], k) for k in range(1, 4)]
    h1, qkv, lse, context, g_out = call(
        forward_kernel,
        "attention_forward",
        (me, xhat, dys, w_qkv, vectors, *tables),
        (scalar, *[None] * 7),
        [(wide, BF), ((1024, 576), BF), ((8, 1024), F32), ((1024, 192), BF), ((4, 192, 192), BF)],
        [((192, 256), F32)],
    )
    g_out = [g_out[0]] + [swap(g_out[k], k) for k in range(1, 4)]

    grads, part, dx = call(
        backward_kernel,
        "attention_backward",
        (me, xhat, dys, w_qkv, vectors, *w_out, *tables, h1, qkv, lse, context, part, dx2, sums),
        (scalar, *[None] * 18),
        [((768, 640), BF), (wide, BF), (wide, BF)],
        [
            ((1024, 192), BF),
            ((192, 1024), F32),
            ((1024, 192), F32),
            ((1024, 192), F32),
            ((1024, 576), BF),
            ((128, 768), F32),
            ((4, 192, 192), BF),
            ((192, 768), BF),
        ],
    )
    g_out = [
        jnp.where(s < 2, jnp.where(s == 0, g_out[c], g_out[c ^ 1]), jnp.where(s == 2, g_out[c ^ 2], g_out[c ^ 3]))
        for c in range(4)
    ]
    grads = jnp.concatenate([grads, jnp.concatenate(g_out)], axis=1)
    grads, plane_first, part, dx = lax.optimization_barrier((grads, plane_first, part, dx))
    plane_second = plane_exchange(grads)
    part = part.reshape(2, 2, 256, 768)
    block_output = (x.astype(F32) + seq_reduce(part[:, 0], part[:, 1])).astype(BF)
    dx = dx.reshape(2, 2, 256, 768)
    dxhat = seq_reduce(dx[:, 0], dx[:, 1])
    xhat, rstd = xhat[:256], rstd[:256]
    dxhat = dxhat - jnp.mean(dxhat, axis=-1, keepdims=True) - xhat * jnp.mean(dxhat * xhat, axis=-1, keepdims=True)
    input_grad = (dy.astype(F32) + rstd * dxhat).astype(BF)

    every = lax.all_gather(pair_sum(plane_sum(plane_first)), "seq", axis=0)
    t_up, t_down = call(first_kernel, "place_first", (every,), (None,), [((24, 3072), F32), ((96, 768), F32)])
    plane_second, t_up = lax.optimization_barrier((plane_second, t_up))
    sum_second = pair_sum(plane_sum(plane_second))
    every = lax.all_gather(sum_second, "seq", axis=0)
    t_qkv, t_out, g_g1, g_b1, g_g2, g_b2, g_b, g_qkvb, g_upb = call(
        second_kernel,
        "place_second",
        (every,),
        (None,),
        [((24, 2304), F32), ((24, 768), F32), *[((24,), F32)] * 5, ((72,), F32), ((96,), F32)],
    )
    return (
        block_output[None],
        input_grad[None],
        g_g1,
        g_b1,
        g_g2,
        g_b2,
        t_qkv,
        g_qkvb,
        t_out,
        g_b,
        t_up,
        g_upb,
        t_down,
        g_b,
    )


def solution(mesh):
    rows, vector, weight = P("dp", "seq", None), P("dp"), P("dp", None)
    params = (vector, vector, vector, vector, weight, vector, weight, vector, weight, vector, weight, vector)
    return jax.shard_map(
        per_device,
        mesh=mesh,
        in_specs=(rows, rows, *params),
        out_specs=(rows, rows, *params),
        check_vma=False,
    )
```

```python
import jax
import jax.numpy as jnp
from jax import lax
from jax.experimental import pallas as pl
from jax.experimental.pallas import tpu as pltpu
from jax.sharding import PartitionSpec as P

HD = 64
ROT = 16
F32 = jnp.float32
BF = jnp.bfloat16


def swap(value, bits):
    return lax.ppermute(value, "seq", [(s, s ^ bits) for s in range(4)])


def seq_gather(value, earlier):
    far = swap(value, 2)
    sent, *_ = lax.optimization_barrier((far, *earlier))
    return [swap(value, 1), far, swap(sent, 1)]


def seq_sum(kept, sent):
    core = swap(sent, 1).astype(F32)
    far = (kept[1].astype(F32) + core[1]).astype(BF)
    return kept[0].astype(F32) + core[0] + swap(far, 2).astype(F32)


def dp_groups():
    return [[2 * p + z for p in range(16)] for z in range(2)]


def plane_exchange(parts):
    return lax.all_to_all(
        parts.reshape(16, 48, -1), "dp", split_axis=0, concat_axis=0, tiled=True, axis_index_groups=dp_groups()
    )


def dp_shift(value, along_y, along_x):
    pairs = []
    for d in range(32):
        y, x, z = d // 8, d // 2 % 4, d % 2
        pairs.append((d, ((y + along_y) % 4 * 4 + (x + along_x) % 4) * 2 + z))
    return lax.ppermute(value, "dp", pairs)


def across_pair(value):
    return lax.ppermute(value, "dp", [(d, d ^ 1) for d in range(32)])


SOURCES = (0, -1, 1, 2)


def line_gather(value, along):
    lines = [[2 * p + z for p in range(16) if (p // 4, p % 4)[along == "y"] == fixed] for fixed in range(4) for z in range(2)]
    copies = jnp.broadcast_to(value[None], (4, *value.shape))
    got = lax.all_to_all(copies, "dp", split_axis=0, concat_axis=0, tiled=True, axis_index_groups=lines)
    return got.reshape(4 * value.shape[0], -1)


def dp_gather(shard, other, cut):
    low = lax.axis_index("dp") % 2 == 0
    pair = jnp.concatenate([jnp.where(low, shard, other), jnp.where(low, other, shard)], axis=0)
    left, right = [pair[:, :cut]], [pair[:, cut:]]
    for step in (1, 2, 3):
        left.append(dp_shift(left[0], 0, -step))
        right.append(dp_shift(right[0], -SOURCES[step], 0))
    x = lax.axis_index("dp") // 2 % 4
    left = jnp.concatenate(
        [
            jnp.where(
                x < 2,
                jnp.where(x == 0, left[c], left[(c + 3) % 4]),
                jnp.where(x == 2, left[(c + 2) % 4], left[(c + 1) % 4]),
            )
            for c in range(4)
        ]
    )
    y, s = lax.axis_index("dp") // 8, lax.axis_index("seq")
    rows = right[0][:, 1024:]
    for step in (1, 2, 3):
        rows = jnp.where((y + SOURCES[step]) % 4 == s, right[step][:, 1024:], rows)
    rows = jnp.concatenate([rows[:, at : at + 192] for at in range(0, 768, 192)])
    right = [jnp.concatenate([jnp.concatenate([r[:, :1024] for r in right]), rows], axis=1)]
    for step in SOURCES[1:]:
        right.append(dp_shift(right[0], 0, -step))
    return line_gather(left, "y"), right


def plane_sum(parts):
    return jnp.sum(parts.astype(F32), axis=0)


def pair_sum(total):
    half = lax.axis_index("dp") % 2
    kept = lax.dynamic_slice_in_dim(total, half * 24, 24, 0)
    sent = lax.dynamic_slice_in_dim(total, (1 - half) * 24, 24, 0).astype(BF)
    return (kept + across_pair(sent).astype(F32)).astype(BF)


def normalize(x):
    average = jnp.mean(x, axis=-1, keepdims=True)
    centered = x - average
    spread = jnp.mean(centered * centered, axis=-1, keepdims=True)
    rstd = lax.rsqrt(spread + 1e-05)
    return centered * rstd, rstd


def dot(a, b, ca=1, cb=0):
    return lax.dot_general(a, b, (((ca,), (cb,)), ((), ())), preferred_element_type=F32)


def rotary_tables(position):
    at = jnp.arange(2 * HD) % HD
    frequency = 10000.0 ** (-2.0 * (at % (ROT // 2)).astype(F32) / ROT)
    angles = position.astype(F32)[:, None] * frequency[None, :]
    own = jnp.where(at < ROT, jnp.cos(angles), 1.0)
    sine = jnp.sin(angles)
    above = jnp.where(at < ROT // 2, -sine, 0.0)
    below = jnp.where((at >= ROT // 2) & (at < ROT), sine, 0.0)
    return own, above, below


def turn(block, own, above, below):
    columns = []
    for at in range(0, 384, 128):
        part = block[:, at : at + 128]
        columns.append(part * own + pltpu.roll(part, 120, 1) * above + pltpu.roll(part, 8, 1) * below)
    return jnp.concatenate(columns, -1)


def causal(shape):
    return lax.broadcasted_iota(jnp.int32, shape, 0) <= lax.broadcasted_iota(jnp.int32, shape, 1)


def by24(index):
    return jnp.floor((index.astype(F32) + 0.5) * (1.0 / 24.0)).astype(jnp.int32)


def lane(n):
    return lax.broadcasted_iota(jnp.int32, (1, n), 1)


def sublane(n):
    return lax.broadcasted_iota(jnp.int32, (n, 1), 0)


def one_hot(rows, columns):
    return jnp.where(rows == columns, 1.0, 0.0).astype(BF)


def bias_places(me):
    column = sublane(576)
    column = column + 576 * ((column >= 192).astype(jnp.int32) + (column >= 384).astype(jnp.int32)) + 192 * me
    target = lane(768)
    target = target + 48 * by24(target)
    return [one_hot(column, target + 24 * third) for third in range(3)]


def pack_kernel(seq, wqkv, wo, wu, wd, g1, b1, g2, b2, bo, bd, bu, bqkv, out):
    me = seq[0]

    def chosen(pieces):
        result = pieces[0]
        for at in range(1, 4):
            result = jnp.where(me == at, pieces[at], result)
        return result

    target = lane(384)
    target = target + 72 * by24(target) + 24 * me
    pick = one_hot(sublane(1536), target)
    up = [dot(wu[:, 0:1536], pick), dot(wu[:, 1536:3072], pick)]
    rows = wd[...].astype(F32)
    down = chosen([rows[24 * q : 24 * q + 24] for q in range(4)])
    columns = wqkv[...].astype(F32)
    qkv = [chosen([columns[:, k + 192 * q : k + 192 * q + 192] for q in range(4)]) for k in (0, 768, 1536)]
    outs = wo[...].astype(F32)
    rows = [ref[...].astype(F32).reshape(1, 24) for ref in (g1, b1, g2, b2, bo, bd)]
    bias = bu[...].astype(F32).reshape(1, 96)
    rows.append(chosen([bias[:, 24 * q : 24 * q + 24] for q in range(4)]))
    bias = bqkv[...].astype(F32).reshape(1, 72)
    rows += [bias[:, 24 * q : 24 * q + 24] for q in range(3)]
    vectors = jnp.concatenate(rows + [jnp.zeros((6, 24), F32)], axis=0)
    vectors = jnp.concatenate([vectors, jnp.zeros((16, 104), F32)], axis=1)
    vectors = jnp.concatenate([vectors, jnp.zeros((112, 128), F32)], axis=0).T[0:24, 0:64]
    out[...] = jnp.concatenate([*up, *qkv[:2], down, qkv[2], vectors, outs], axis=1).astype(BF)


def normal(rows):
    rows = rows.astype(F32)
    centered = rows - jnp.mean(rows, axis=-1, keepdims=True)
    spread = jnp.mean(centered * centered, axis=-1, keepdims=True)
    return centered * lax.rsqrt(spread + 1e-05)


def rows_of(place, outer, inner):
    one = lax.rem(place[1] + (SOURCES[inner] + 4), 4) * 4 + lax.rem(place[2] + (SOURCES[outer] + 4), 4)
    return pl.ds(pl.multiple_of(one * 48, 48), 48)


def mlp_kernel(
    place, x_own, dy_own, core, opposite, across, wu, right_0, right_1, right_2, right_3,
    part_far, grads, sums, dx_far, wv, wo, vectors, xs_far, dy_far,
    h2_s, act_s, dup_s, wd, vec_s, part, dx, xs, dy, moved,
):
    own = [(x_own, xs, 0, 0), (dy_own, dy, 0, 0)]
    for at, ref in enumerate((core, opposite, across)):
        own += [(ref, xs, 0, at + 1), (ref, dy, 256, at + 1)]
    loads = [
        pltpu.make_async_copy(ref.at[first : first + 256], to.at[256 * at : 256 * at + 256], moved.at[k])
        for k, (ref, to, first, at) in enumerate(own)
    ]
    for load in loads:
        load.start()
    for outer, right in enumerate((right_0, right_1, right_2, right_3)):
        for inner in range(4):
            rows = rows_of(place, outer, inner)
            piece = right[inner * 48 : inner * 48 + 48, :]
            wd[rows, :] = piece[:, 0:768]
            wv[rows, :] = piece[:, 768:960]
            vec_s[rows, 0:64] = piece[:, 960:1024].astype(F32)
            rows = pl.ds(pl.multiple_of(lax.rem(place[2] + (SOURCES[outer] + 4), 4) * 48, 48), 48)
            wo[rows, 192 * inner : 192 * inner + 192] = piece[:, 1024:1216]
    vectors[...] = vec_s[...].T[0:16]
    for load in loads:
        load.wait()
    stores = [
        pltpu.make_async_copy(ref, to, moved.at[8 + k])
        for k, (ref, to) in enumerate(((xs, xs_far), (dy, dy_far), (part, part_far), (dx, dx_far)))
    ]
    stores[0].start()
    stores[1].start()
    sums[...] = jnp.zeros_like(sums)

    @pl.loop(0, 4)
    def _(step):
        rows = pl.ds(pl.multiple_of(step * 256, 256), 256)
        xh = normal(xs[rows, :])
        gain = vectors[2:3, :]
        h2 = (xh * gain + vectors[3:4, :]).astype(BF)
        h2_s[rows, :] = h2
        upper = dot(h2, wu[...]) + vectors[6:7, :]
        phi = 0.5 + 0.5 * lax.erf(upper * 0.7071067811865476)
        active = (upper * phi).astype(BF)
        act_s[rows, :] = active
        slope = phi + upper * (jnp.exp(-0.5 * upper * upper) * 0.3989422804014327)
        dup = (dot(dy[rows, :], wd[...], 1, 1) * slope).astype(BF)
        dup_s[rows, :] = dup
        part[rows, :] = dot(active, wd[...]).astype(BF)
        dh2 = dot(dup, wu[...], 1, 1)
        dx[rows, :] = (dh2 * gain).astype(BF)
        sums[0:1, :] += jnp.sum(dh2 * xh, axis=0, keepdims=True)
        sums[1:2, :] += jnp.sum(dh2, axis=0, keepdims=True)
        sums[2:3, :] += jnp.sum(dup.astype(F32), axis=0, keepdims=True)

    stores[2].start()
    stores[3].start()
    for at in range(0, 768, 256):
        grads[at : at + 256, 0:768] = dot(h2_s[:, at : at + 256], dup_s[...], 0, 0).astype(BF)
        grads[at : at + 256, 768:1536] = dot(act_s[:, at : at + 256], dy[...], 0, 0).astype(BF)
    for store in stores:
        store.wait()


def forward_kernel(
    seq, xs, dy, wqk, wv, vec_s, wo, own, above, below, before,
    qkv, lse, out_0, out_1, out_2, out_3, part_kept, part_sent, ctx_s, total, pieces, part
):
    me = seq[0]
    bias_out = jnp.where(me == 0, vec_s[4:5, :] + vec_s[5:6, :], 0.0)
    bias_qkv = jnp.zeros((1, 576), F32)
    for third, place in enumerate(bias_places(me)):
        bias_qkv += dot(vec_s[7 + third : 8 + third, :].astype(BF), place, 1, 1)

    @pl.loop(0, 4)
    def _(step):
        rows = pl.ds(pl.multiple_of(step * 256, 256), 256)
        place = pl.ds(pl.multiple_of((step ^ me) * 256, 256), 256)
        h = (normal(xs[rows, :]) * vec_s[0:1, :] + vec_s[1:2, :]).astype(BF)
        mixed = dot(h, wqk[...]) + bias_qkv[:, 0:384]
        qkv[place, 0:384] = turn(mixed, own[rows, :], above[rows, :], below[rows, :]).astype(BF)
        qkv[place, 384:576] = (dot(h, wv[...]) + bias_qkv[:, 384:576]).astype(BF)

    allowed = causal((256, 256))
    for block in range(4):
        first, keys = block * 256, block * 256 + 256
        for head in range(3):
            at = head * 64
            query = qkv[first:keys, at : at + 64] * 0.125
            scores = dot(qkv[0:keys, 192 + at : 256 + at], query, 1, 1)
            last = jnp.where(allowed, scores[first:], -1e30)
            scores = jnp.concatenate([scores[:first], last], 0) if block else last
            top = jnp.max(scores, axis=0, keepdims=True)
            weight = jnp.exp(scores - top)
            count = jnp.sum(weight, axis=0, keepdims=True)
            lse[head : head + 1, first:keys] = top + jnp.log(count)
            context = dot(qkv[0:keys, 384 + at : 448 + at], weight.astype(BF), 0, 0)
            ctx_s[at : at + 64, :] = context / count
        place = pl.ds(pl.multiple_of((me ^ block) * 256, 256), 256)
        context = ctx_s[...].T.astype(BF)
        total[place, :] = context
        part[me ^ block] = (before[place, :].astype(F32) + dot(context, wo[...]) + bias_out).astype(BF)
    rows = dot(total[...], dy[...], 0, 0)
    for column in range(4):
        pieces[column] = rows[:, 192 * column : 192 * column + 192].astype(BF)
    for at, ref in enumerate((out_0, out_1, out_2, out_3)):
        ref[:, 0:192] = pieces[at ^ me]
        ref[:, 192:256] = jnp.zeros((192, 64), BF)
    for at in range(4):
        (part_sent if at % 2 else part_kept)[at // 2] = part[at]


def backward_kernel(
    seq, xs_far, dy, wqk, wv, vec_s, wo, own, above, below, qkv, lse, dx2_far, sums,
    grads, dx_kept, dx_sent, do_s, dq_s, dk_s, dv_s, dm_s, sum_s, h1_s, xs, dx2, arrived,
):
    me = seq[0]
    load_xs = pltpu.make_async_copy(xs_far, xs, arrived.at[0])
    load_dx2 = pltpu.make_async_copy(dx2_far, dx2, arrived.at[1])
    load_xs.start()
    load_dx2.start()
    sum_s[...] = jnp.zeros_like(sum_s)

    @pl.loop(0, 4)
    def _(step):
        rows = pl.ds(pl.multiple_of(step * 256, 256), 256)
        place = pl.ds(pl.multiple_of((step ^ me) * 256, 256), 256)
        do_s[place, :] = dot(dy[rows, :], wo[...], 1, 1).astype(BF)

    allowed = causal((256, 256))
    for block in reversed(range(4)):
        first, keys = block * 256, block * 256 + 256
        for head in range(3):
            at = head * 64
            query = qkv[first:keys, at : at + 64] * 0.125
            key = qkv[0:keys, 192 + at : 256 + at]
            dcontext = do_s[first:keys, at : at + 64]
            scores = dot(key, query, 1, 1)
            last = jnp.where(allowed, scores[first:], -1e30)
            scores = jnp.concatenate([scores[:first], last], 0) if block else last
            probs = jnp.exp(scores - lse[head : head + 1, first:keys])
            dprobs = dot(qkv[0:keys, 384 + at : 448 + at], dcontext, 1, 1)
            delta = jnp.sum(probs * dprobs, axis=0, keepdims=True)
            dscores = (probs * (dprobs - delta)).astype(BF)
            dv = dot(probs.astype(BF), dcontext)
            dk = dot(dscores, query)
            if block == 3:
                dv_s[:, at : at + 64] = dv
                dk_s[:, at : at + 64] = dk
            else:
                dv_s[0:keys, at : at + 64] += dv
                dk_s[0:keys, at : at + 64] += dk
            dq_s[at : at + 64, first:keys] = dot(key, dscores, 0, 0) * 0.125

    for block in range(4):
        first, keys = block * 256, block * 256 + 256
        place = pl.ds(pl.multiple_of((me ^ block) * 256, 256), 256)
        both = jnp.concatenate([dq_s[:, first:keys].T, dk_s[first:keys, :]], -1)
        both = both.astype(BF).astype(F32)
        both = turn(both, own[place, :], -above[place, :], -below[place, :])
        dm_s[place, 0:384] = both.astype(BF)
        dm_s[place, 384:576] = dv_s[first:keys, :].astype(BF)

    load_xs.wait()
    load_dx2.wait()
    bias_qkv = jnp.zeros((1, 576), F32)
    for step in range(4):
        rows = slice(step * 256, step * 256 + 256)
        dmixed = dm_s[rows, :]
        xh = normal(xs[rows, :])
        h1_s[rows, :] = (xh * vec_s[0:1, :] + vec_s[1:2, :]).astype(BF)
        dh1 = dot(dmixed[:, 0:384], wqk[...], 1, 1) + dot(dmixed[:, 384:576], wv[...], 1, 1)
        (dx_sent if step % 2 else dx_kept)[step // 2] = (dh1 * vec_s[0:1, :] + dx2[rows, :].astype(F32)).astype(BF)
        bias_qkv += jnp.sum(dmixed.astype(F32), axis=0, keepdims=True)
        sum_s[0:1, :] += jnp.sum(dh1 * xh, axis=0, keepdims=True)
        sum_s[1:2, :] += jnp.sum(dh1, axis=0, keepdims=True)
    sum_s[2:4, :] = sums[0:2, :]
    sum_s[4:5, :] = jnp.sum(dy[0:256, :].astype(F32), axis=0, keepdims=True)
    sum_s[5:6, :] = sums[2:3, :]
    for third, place in enumerate(bias_places(me)):
        sum_s[6 + third : 7 + third, :] = dot(bias_qkv.astype(BF), place)
    columns = sum_s[...].T[:, 0:64]
    for at in range(0, 768, 256):
        chunk = dot(h1_s[:, at : at + 256], dm_s[...], 0, 0)
        grads[at : at + 256, 256:896] = jnp.concatenate([chunk, columns[at : at + 256]], -1).astype(BF)


def join_kernel(seq, grads, out_0, out_1, out_2, out_3, joined):
    for at, piece in enumerate((out_0, out_1, out_2, out_3)):
        joined[pl.ds(pl.multiple_of((seq[0] ^ at) * 192, 192), 192), :] = piece[...]


def place_kernel(every, up, down, qkv, out, *small):
    row = sublane(384)
    group = jnp.floor((row.astype(F32) + 0.5) * (1.0 / 96.0)).astype(jnp.int32)
    inner = row - 96 * group
    pick = one_hot(inner + 72 * by24(inner) + 24 * group, lane(384))
    parts = [every[at].astype(F32) for at in range(4)]
    for at in range(8):
        columns = jnp.concatenate([p[:, 96 * at : 96 * at + 96] for p in parts], -1).astype(BF)
        up[:, 384 * at : 384 * at + 384] = dot(columns, pick)
    down[...] = jnp.concatenate([p[:, 768:1536] for p in parts], 0)
    for kind in range(3):
        qkv[:, 768 * kind : 768 * kind + 768] = jnp.concatenate(
            [p[:, 1792 + 192 * kind : 1984 + 192 * kind] for p in parts], -1
        )
    out[...] = jnp.concatenate([p[:, 1536:1728] for p in parts], -1)
    pad = jnp.zeros((104, 64), F32)
    rows = [jnp.concatenate([p[:, 2368:2432], pad], 0).T for p in parts]
    total = rows[0] + rows[1] + rows[2] + rows[3]
    for at, ref in zip((0, 1, 2, 3, 4, 4), small):
        ref[...] = total[at, 0:24]
    small[6][...] = jnp.concatenate([total[at : at + 1, 0:24] for at in (6, 7, 8)], -1)[0]
    small[7][...] = jnp.concatenate([r[5:6, 0:24] for r in rows], -1)[0]


def whole(shape):
    return pl.BlockSpec(shape, lambda i: (0,) * len(shape))


def call(kernel, name, args, specs, outs, scratch=(), far=()):
    shapes = [jax.ShapeDtypeStruct(shape, dtype) for shape, dtype in outs]
    return pl.pallas_call(
        kernel,
        name=name,
        grid=(1,),
        in_specs=[whole(a.shape) if spec is None else spec for a, spec in zip(args, specs)],
        out_specs=[
            pl.BlockSpec(memory_space=pl.ANY) if at in far else whole(shape.shape) for at, shape in enumerate(shapes)
        ],
        out_shape=shapes,
        scratch_shapes=[pltpu.VMEM(*s) if isinstance(s, tuple) else s for s in scratch],
        cost_estimate=pl.CostEstimate(flops=1_000_000, bytes_accessed=100_000, transcendentals=0),
        compiler_params=pltpu.CompilerParams(vmem_limit_bytes=56 * 2**20),
    )(*args)


def per_device(x, dy, g1, b1, g2, b2, wqkv, bqkv, wo, bo, wu, bu, wd, bd):
    s = lax.axis_index("seq")
    d = lax.axis_index("dp").astype(jnp.int32)
    me = s.astype(jnp.int32).reshape(1)
    place = jnp.stack([s.astype(jnp.int32), d // 8, d // 2 % 4])
    scalar, far = pl.BlockSpec(memory_space=pltpu.SMEM), pl.BlockSpec(memory_space=pl.ANY)
    x, dy = x[0], dy[0]
    (packed,) = call(
        pack_kernel,
        "pack",
        (me, wqkv, wo, wu, wd, g1, b1, g2, b2, bo, bd, bu, bqkv),
        (scalar, *[None] * 12),
        [((24, 2944), BF)],
    )
    other, both = lax.optimization_barrier((across_pair(packed), jnp.concatenate([x, dy])))
    left, right = dp_gather(packed, other, 1152)

    position = jnp.concatenate([(s ^ k) * 256 + jnp.arange(256, dtype=jnp.int32) for k in range(4)])
    tables = rotary_tables(position)
    blocks = seq_gather(both, right[1:])

    wide, tall, lines = (1024, 768), ((1024, 768), BF), ((16, 768), F32)
    blocks[0], *tables = lax.optimization_barrier((blocks[0], *tables))
    part, grads, sums, dx2, w_v, w_out, vectors, xs, dys = call(
        mlp_kernel,
        "mlp",
        (place, x, dy, *blocks, left, *right),
        (scalar, *[far] * 5, whole((768, 768)), *[None] * 4),
        [(wide, BF), ((768, 1536), BF), ((8, 768), F32), (wide, BF), ((768, 192), BF), ((192, 768), BF), lines, (wide, BF), (wide, BF)],
        [
            *[tall] * 3,
            ((768, 768), BF),
            ((768, 128), F32),
            *[tall] * 4,
            pltpu.SemaphoreType.DMA((12,)),
        ],
        (0, 3, 7, 8),
    )
    plane_first = plane_exchange(grads)
    w_qk = pl.BlockSpec((768, 384), lambda i: (0, 2))
    qkv, lse, *pieces = call(
        forward_kernel,
        "attention_forward",
        (me, xs, dys, left, w_v, vectors, w_out, *tables, part),
        (scalar, None, None, w_qk, *[None] * 7),
        [((1024, 576), BF), ((8, 1024), F32), *[((192, 256), BF)] * 4, *[((2, 256, 768), BF)] * 2],
        [((192, 256), F32), ((1024, 192), BF), ((4, 192, 192), BF), ((4, 256, 768), BF)],
    )
    g_out, part = pieces[:4], pieces[4:]
    g_out = [g_out[0]] + [swap(g_out[k], k) for k in range(1, 4)]

    grads, dx_kept, dx_sent = call(
        backward_kernel,
        "attention_backward",
        (me, xs, dys, left, w_v, vectors, w_out, *tables, qkv, lse, dx2, sums),
        (scalar, far, None, w_qk, *[None] * 8, far, None),
        [((768, 896), BF), ((2, 256, 768), BF), ((2, 256, 768), BF)],
        [
            ((1024, 192), BF),
            ((192, 1024), F32),
            ((1024, 192), F32),
            ((1024, 192), F32),
            ((1024, 576), BF),
            ((128, 768), F32),
            tall,
            tall,
            tall,
            pltpu.SemaphoreType.DMA((2,)),
        ],
    )
    grads = pl.pallas_call(
        join_kernel,
        name="join",
        grid=(1,),
        in_specs=[scalar, far, *[whole((192, 256))] * 4],
        out_specs=pl.BlockSpec((768, 256), lambda i: (0, 0)),
        out_shape=jax.ShapeDtypeStruct((768, 896), BF),
        input_output_aliases={1: 0},
        cost_estimate=pl.CostEstimate(flops=1_000_000, bytes_accessed=100_000, transcendentals=0),
    )(me, grads, *g_out)
    grads, plane_first, dx_kept, dx_sent, *part = lax.optimization_barrier(
        (grads, plane_first, dx_kept, dx_sent, *part)
    )
    plane_second = plane_exchange(grads)
    block_output = (x.astype(F32) + seq_sum(*part)).astype(BF)
    dxhat = seq_sum(dx_kept, dx_sent)
    xhat, rstd = normalize(x.astype(F32))
    dxhat = dxhat - jnp.mean(dxhat, axis=-1, keepdims=True) - xhat * jnp.mean(dxhat * xhat, axis=-1, keepdims=True)
    input_grad = (dy.astype(F32) + rstd * dxhat).astype(BF)
    plane_first, plane_second = lax.optimization_barrier((plane_first, plane_second))
    sums = jnp.concatenate([plane_sum(plane_first), plane_sum(plane_second)], axis=1)
    every = lax.all_gather(pair_sum(sums), "seq", axis=0)
    t_up, t_down, t_qkv, t_out, g_g1, g_b1, g_g2, g_b2, g_bo, g_bd, g_qkvb, g_upb = call(
        place_kernel,
        "place",
        (every,),
        (None,),
        [
            ((24, 3072), F32),
            ((96, 768), F32),
            ((24, 2304), F32),
            ((24, 768), F32),
            *[((24,), F32)] * 6,
            ((72,), F32),
            ((96,), F32),
        ],
    )
    return (
        block_output[None],
        input_grad[None],
        g_g1,
        g_b1,
        g_g2,
        g_b2,
        t_qkv,
        g_qkvb,
        t_out,
        g_bo,
        t_up,
        g_upb,
        t_down,
        g_bd,
    )


def solution(mesh):
    rows, vector, weight = P("dp", "seq", None), P("dp"), P("dp", None)
    params = (vector, vector, vector, vector, weight, vector, weight, vector, weight, vector, weight, vector)
    return jax.shard_map(
        per_device,
        mesh=mesh,
        in_specs=(rows, rows, *params),
        out_specs=(rows, rows, *params),
        check_vma=False,
    )
```

```python
import jax
import jax.numpy as jnp
from jax import lax
from jax.experimental import pallas as pl
from jax.experimental.pallas import tpu as pltpu
from jax.sharding import PartitionSpec as P

HD = 64
ROT = 16
F32 = jnp.float32
BF = jnp.bfloat16


def swap(value, bits):
    return lax.ppermute(value, "seq", [(s, s ^ bits) for s in range(4)])


def seq_gather(value, earlier):
    far = swap(value, 2)
    sent, *_ = lax.optimization_barrier((far, *earlier))
    return [swap(value, 1), far, swap(sent, 1)]


def seq_sum(kept, sent):
    return seq_rest(kept, swap(sent, 1))


def seq_rest(kept, core):
    core = core.astype(F32)
    far = (kept[1].astype(F32) + core[1]).astype(BF)
    return kept[0].astype(F32) + core[0] + swap(far, 2).astype(F32)


def dp_groups():
    return [[2 * p + z for p in range(16)] for z in range(2)]


def plane_exchange(parts):
    return lax.all_to_all(
        parts.reshape(16, 48, -1), "dp", split_axis=0, concat_axis=0, tiled=True, axis_index_groups=dp_groups()
    )


def dp_shift(value, along_y, along_x):
    pairs = []
    for d in range(32):
        y, x, z = d // 8, d // 2 % 4, d % 2
        pairs.append((d, ((y + along_y) % 4 * 4 + (x + along_x) % 4) * 2 + z))
    return lax.ppermute(value, "dp", pairs)


def across_pair(value):
    return lax.ppermute(value, "dp", [(d, d ^ 1) for d in range(32)])


SOURCES = (0, -1, 1, 2)


def line_gather(value, along):
    lines = [[2 * p + z for p in range(16) if (p // 4, p % 4)[along == "y"] == fixed] for fixed in range(4) for z in range(2)]
    copies = jnp.broadcast_to(value[None], (4, *value.shape))
    got = lax.all_to_all(copies, "dp", split_axis=0, concat_axis=0, tiled=True, axis_index_groups=lines)
    return got.reshape(4 * value.shape[0], -1)


def dp_gather(shard, other, cut):
    low = lax.axis_index("dp") % 2 == 0
    pair = jnp.concatenate([jnp.where(low, shard, other), jnp.where(low, other, shard)], axis=0)
    left, right = [pair[:, :cut]], [pair[:, cut:]]
    for step in (1, 2, 3):
        left.append(dp_shift(left[0], 0, -step))
        right.append(dp_shift(right[0], -SOURCES[step], 0))
    x = lax.axis_index("dp") // 2 % 4
    left = jnp.concatenate(
        [
            jnp.where(
                x < 2,
                jnp.where(x == 0, left[c], left[(c + 3) % 4]),
                jnp.where(x == 2, left[(c + 2) % 4], left[(c + 1) % 4]),
            )
            for c in range(4)
        ]
    )
    y, s = lax.axis_index("dp") // 8, lax.axis_index("seq")
    rows = right[0][:, 1024:]
    for step in (1, 2, 3):
        rows = jnp.where((y + SOURCES[step]) % 4 == s, right[step][:, 1024:], rows)
    rows = jnp.concatenate([rows[:, at : at + 192] for at in range(0, 768, 192)])
    right = [jnp.concatenate([jnp.concatenate([r[:, :1024] for r in right]), rows], axis=1)]
    for step in SOURCES[1:]:
        right.append(dp_shift(right[0], 0, -step))
    return line_gather(left, "y"), right


def plane_sum(parts):
    return jnp.sum(parts.astype(F32), axis=0)


def pair_sum(total):
    half = lax.axis_index("dp") % 2
    kept = lax.dynamic_slice_in_dim(total, half * 24, 24, 0)
    sent = lax.dynamic_slice_in_dim(total, (1 - half) * 24, 24, 0).astype(BF)
    return (kept + across_pair(sent).astype(F32)).astype(BF)


def normalize(x):
    average = jnp.mean(x, axis=-1, keepdims=True)
    centered = x - average
    spread = jnp.mean(centered * centered, axis=-1, keepdims=True)
    rstd = lax.rsqrt(spread + 1e-05)
    return centered * rstd, rstd


def dot(a, b, ca=1, cb=0):
    return lax.dot_general(a, b, (((ca,), (cb,)), ((), ())), preferred_element_type=F32)


def rotary_tables(position):
    at = jnp.arange(2 * HD) % HD
    frequency = 10000.0 ** (-2.0 * (at % (ROT // 2)).astype(F32) / ROT)
    angles = position.astype(F32)[:, None] * frequency[None, :]
    own = jnp.where(at < ROT, jnp.cos(angles), 1.0)
    sine = jnp.sin(angles)
    above = jnp.where(at < ROT // 2, -sine, 0.0)
    below = jnp.where((at >= ROT // 2) & (at < ROT), sine, 0.0)
    return own, above, below


def turn(block, own, above, below):
    columns = []
    for at in range(0, 384, 128):
        part = block[:, at : at + 128]
        columns.append(part * own + pltpu.roll(part, 120, 1) * above + pltpu.roll(part, 8, 1) * below)
    return jnp.concatenate(columns, -1)


def causal(shape):
    return lax.broadcasted_iota(jnp.int32, shape, 0) <= lax.broadcasted_iota(jnp.int32, shape, 1)


def by24(index):
    return jnp.floor((index.astype(F32) + 0.5) * (1.0 / 24.0)).astype(jnp.int32)


def lane(n):
    return lax.broadcasted_iota(jnp.int32, (1, n), 1)


def sublane(n):
    return lax.broadcasted_iota(jnp.int32, (n, 1), 0)


def one_hot(rows, columns):
    return jnp.where(rows == columns, 1.0, 0.0).astype(BF)


def bias_places(me):
    column = sublane(576)
    column = column + 576 * ((column >= 192).astype(jnp.int32) + (column >= 384).astype(jnp.int32)) + 192 * me
    target = lane(768)
    target = target + 48 * by24(target)
    return [one_hot(column, target + 24 * third) for third in range(3)]


def pack_kernel(seq, wqkv, wo, wu, wd, g1, b1, g2, b2, bo, bd, bu, bqkv, out):
    me = seq[0]

    def chosen(pieces):
        result = pieces[0]
        for at in range(1, 4):
            result = jnp.where(me == at, pieces[at], result)
        return result

    target = lane(384)
    target = target + 72 * by24(target) + 24 * me
    pick = one_hot(sublane(1536), target)
    up = [dot(wu[:, 0:1536], pick), dot(wu[:, 1536:3072], pick)]
    rows = wd[...].astype(F32)
    down = chosen([rows[24 * q : 24 * q + 24] for q in range(4)])
    columns = wqkv[...].astype(F32)
    qkv = [chosen([columns[:, k + 192 * q : k + 192 * q + 192] for q in range(4)]) for k in (0, 768, 1536)]
    outs = wo[...].astype(F32)
    rows = [ref[...].astype(F32).reshape(1, 24) for ref in (g1, b1, g2, b2, bo, bd)]
    bias = bu[...].astype(F32).reshape(1, 96)
    rows.append(chosen([bias[:, 24 * q : 24 * q + 24] for q in range(4)]))
    bias = bqkv[...].astype(F32).reshape(1, 72)
    rows += [bias[:, 24 * q : 24 * q + 24] for q in range(3)]
    vectors = jnp.concatenate(rows + [jnp.zeros((6, 24), F32)], axis=0)
    vectors = jnp.concatenate([vectors, jnp.zeros((16, 104), F32)], axis=1)
    vectors = jnp.concatenate([vectors, jnp.zeros((112, 128), F32)], axis=0).T[0:24, 0:64]
    out[...] = jnp.concatenate([*up, *qkv[:2], down, qkv[2], vectors, outs], axis=1).astype(BF)


def normal(rows):
    rows = rows.astype(F32)
    centered = rows - jnp.mean(rows, axis=-1, keepdims=True)
    spread = jnp.mean(centered * centered, axis=-1, keepdims=True)
    return centered * lax.rsqrt(spread + 1e-05)


def rows_of(place, outer, inner):
    one = lax.rem(place[1] + (SOURCES[inner] + 4), 4) * 4 + lax.rem(place[2] + (SOURCES[outer] + 4), 4)
    return pl.ds(pl.multiple_of(one * 48, 48), 48)


def mlp_kernel(
    place, x_own, dy_own, core, opposite, across, wu, right_0, right_1, right_2, right_3,
    act_far, grads, sums, dup_far, wv, wo, vectors, xs_far, dy_far, wd_far,
    h2_s, act_s, dup_s, wd, vec_s, xs, dy, moved,
):
    own = [(x_own, xs, 0, 0), (dy_own, dy, 0, 0)]
    for at, ref in enumerate((core, opposite, across)):
        own += [(ref, xs, 0, at + 1), (ref, dy, 256, at + 1)]
    loads = [
        pltpu.make_async_copy(ref.at[first : first + 256], to.at[256 * at : 256 * at + 256], moved.at[k])
        for k, (ref, to, first, at) in enumerate(own)
    ]
    for load in loads:
        load.start()
    for outer, right in enumerate((right_0, right_1, right_2, right_3)):
        for inner in range(4):
            rows = rows_of(place, outer, inner)
            piece = right[inner * 48 : inner * 48 + 48, :]
            wd[rows, :] = piece[:, 0:768]
            wv[rows, :] = piece[:, 768:960]
            vec_s[rows, 0:64] = piece[:, 960:1024].astype(F32)
            rows = pl.ds(pl.multiple_of(lax.rem(place[2] + (SOURCES[outer] + 4), 4) * 48, 48), 48)
            wo[rows, 192 * inner : 192 * inner + 192] = piece[:, 1024:1216]
    vectors[...] = vec_s[...].T[0:16]
    for load in loads:
        load.wait()
    stores = [
        pltpu.make_async_copy(ref, to, moved.at[8 + k])
        for k, (ref, to) in enumerate(((xs, xs_far), (dy, dy_far), (wd, wd_far), (act_s, act_far), (dup_s, dup_far)))
    ]
    for store in stores[:3]:
        store.start()
    sums[...] = jnp.zeros_like(sums)

    @pl.loop(0, 4, unroll=4)
    def _(step):
        rows = pl.ds(pl.multiple_of(step * 256, 256), 256)
        xh = normal(xs[rows, :])
        gain = vectors[2:3, :]
        h2 = (xh * gain + vectors[3:4, :]).astype(BF)
        h2_s[rows, :] = h2
        upper = dot(h2, wu[...]) + vectors[6:7, :]
        phi = 0.5 + 0.5 * lax.erf(upper * 0.7071067811865476)
        active = (upper * phi).astype(BF)
        act_s[rows, :] = active
        slope = phi + upper * (jnp.exp(-0.5 * upper * upper) * 0.3989422804014327)
        dup = (dot(dy[rows, :], wd[...], 1, 1) * slope).astype(BF)
        dup_s[rows, :] = dup
        sums[0:1, :] += jnp.sum(dup.astype(F32), axis=0, keepdims=True)

    stores[3].start()
    stores[4].start()
    for at in range(0, 768, 256):
        grads[at : at + 256, 0:768] = dot(h2_s[:, at : at + 256], dup_s[...], 0, 0).astype(BF)
        grads[at : at + 256, 768:1536] = dot(act_s[:, at : at + 256], dy[...], 0, 0).astype(BF)
    for store in stores:
        store.wait()


def forward_kernel(
    seq, vec_s, *refs
):
    me = seq[0]
    far, (qkv_far, lse, out_0, out_1, out_2, out_3, part_kept, part_sent) = refs[:10], refs[10:18]
    near, (qkv, part, ctx_s, total, pieces, moved) = refs[18:28], refs[28:]
    loads = [pltpu.make_async_copy(far[k], near[k], moved.at[k]) for k in range(10)]
    for load in loads:
        load.start()
    wqk, wv, xs, own, above, below, wd, act, wo, dy = near
    bias_out = jnp.where(me == 0, vec_s[4:5, :] + vec_s[5:6, :], 0.0)
    bias_qkv = jnp.zeros((1, 576), F32)
    for third, place in enumerate(bias_places(me)):
        bias_qkv += dot(vec_s[7 + third : 8 + third, :].astype(BF), place, 1, 1)

    for load in loads[:6]:
        load.wait()

    @pl.loop(0, 4, unroll=2)
    def _(step):
        rows = pl.ds(pl.multiple_of(step * 256, 256), 256)
        place = pl.ds(pl.multiple_of((step ^ me) * 256, 256), 256)
        h = (normal(xs[rows, :]) * vec_s[0:1, :] + vec_s[1:2, :]).astype(BF)
        mixed = dot(h, wqk[:, 768:1152]) + bias_qkv[:, 0:384]
        qkv[place, 0:384] = turn(mixed, own[rows, :], above[rows, :], below[rows, :]).astype(BF)
        qkv[place, 384:576] = (dot(h, wv[...]) + bias_qkv[:, 384:576]).astype(BF)

    store = pltpu.make_async_copy(qkv, qkv_far, moved.at[10])
    store.start()
    for load in loads[6:]:
        load.wait()
    allowed = causal((256, 256))
    for block in range(4):
        first, keys = block * 256, block * 256 + 256
        for head in range(3):
            at = head * 64
            query = qkv[first:keys, at : at + 64] * 0.125
            scores = dot(qkv[0:keys, 192 + at : 256 + at], query, 1, 1)
            last = jnp.where(allowed, scores[first:], -1e30)
            scores = jnp.concatenate([scores[:first], last], 0) if block else last
            top = jnp.max(scores, axis=0, keepdims=True)
            weight = jnp.exp(scores - top)
            count = jnp.sum(weight, axis=0, keepdims=True)
            lse[head : head + 1, first:keys] = top + jnp.log(count)
            context = dot(qkv[0:keys, 384 + at : 448 + at], weight.astype(BF), 0, 0)
            ctx_s[at : at + 64, :] = context / count
        place = pl.ds(pl.multiple_of((me ^ block) * 256, 256), 256)
        context = ctx_s[...].T.astype(BF)
        total[place, :] = context
        part[me ^ block] = (dot(act[place, :], wd[...]) + dot(context, wo[...]) + bias_out).astype(BF)
    stores = [store]
    for at in range(4):
        to = (part_sent if at % 2 else part_kept).at[at // 2]
        stores.append(pltpu.make_async_copy(part.at[at], to, moved.at[11 + at]))
        stores[-1].start()
    rows = dot(total[...], dy[...], 0, 0)
    for column in range(4):
        pieces[column] = rows[:, 192 * column : 192 * column + 192].astype(BF)
    for at, ref in enumerate((out_0, out_1, out_2, out_3)):
        ref[:, 0:192] = pieces[at ^ me]
        ref[:, 192:256] = jnp.zeros((192, 64), BF)
    for store in stores:
        store.wait()


def backward_kernel(
    seq, dy, vec_s, wo, qkv, lse, sums, *refs
):
    me = seq[0]
    far, (grads, kept_far, sent_far) = refs[:7], refs[7:10]
    near, (dx, do_s, dq_s, dk_s, dv_s, dm_s, sum_s, h1_s, moved) = refs[10:17], refs[17:]
    loads = [pltpu.make_async_copy(far[k], near[k], moved.at[k]) for k in range(7)]
    for load in loads:
        load.start()
    own, above, below, left, wv, xs, dup = near
    sum_s[...] = jnp.zeros_like(sum_s)

    @pl.loop(0, 4)
    def _(step):
        rows = pl.ds(pl.multiple_of(step * 256, 256), 256)
        place = pl.ds(pl.multiple_of((step ^ me) * 256, 256), 256)
        do_s[place, :] = dot(dy[rows, :], wo[...], 1, 1).astype(BF)

    allowed = causal((256, 256))
    for block in reversed(range(4)):
        first, keys = block * 256, block * 256 + 256
        for head in range(3):
            at = head * 64
            query = qkv[first:keys, at : at + 64] * 0.125
            key = qkv[0:keys, 192 + at : 256 + at]
            dcontext = do_s[first:keys, at : at + 64]
            scores = dot(key, query, 1, 1)
            last = jnp.where(allowed, scores[first:], -1e30)
            scores = jnp.concatenate([scores[:first], last], 0) if block else last
            probs = jnp.exp(scores - lse[head : head + 1, first:keys])
            dprobs = dot(qkv[0:keys, 384 + at : 448 + at], dcontext, 1, 1)
            delta = jnp.sum(probs * dprobs, axis=0, keepdims=True)
            dscores = (probs * (dprobs - delta)).astype(BF)
            dv = dot(probs.astype(BF), dcontext)
            dk = dot(dscores, query)
            if block == 3:
                dv_s[:, at : at + 64] = dv
                dk_s[:, at : at + 64] = dk
            else:
                dv_s[0:keys, at : at + 64] += dv
                dk_s[0:keys, at : at + 64] += dk
            dq_s[at : at + 64, first:keys] = dot(key, dscores, 0, 0) * 0.125

    for load in loads:
        load.wait()
    for block in range(4):
        first, keys = block * 256, block * 256 + 256
        place = pl.ds(pl.multiple_of((me ^ block) * 256, 256), 256)
        both = jnp.concatenate([dq_s[:, first:keys].T, dk_s[first:keys, :]], -1)
        both = both.astype(BF).astype(F32)
        both = turn(both, own[place, :], -above[place, :], -below[place, :])
        dm_s[place, 0:384] = both.astype(BF)
        dm_s[place, 384:576] = dv_s[first:keys, :].astype(BF)

    stores = []
    bias_qkv = jnp.zeros((1, 576), F32)
    for step in range(4):
        rows = slice(step * 256, step * 256 + 256)
        dmixed = dm_s[rows, :]
        xh = normal(xs[rows, :])
        h1_s[rows, :] = (xh * vec_s[0:1, :] + vec_s[1:2, :]).astype(BF)
        dh1 = dot(dmixed[:, 0:384], left[:, 768:1152], 1, 1) + dot(dmixed[:, 384:576], wv[...], 1, 1)
        dh2 = dot(dup[rows, :], left[:, 0:768], 1, 1)
        dx[step] = (dh1 * vec_s[0:1, :] + dh2 * vec_s[2:3, :]).astype(BF)
        to = (sent_far if step % 2 else kept_far).at[step // 2]
        stores.append(pltpu.make_async_copy(dx.at[step], to, moved.at[7 + step]))
        stores[-1].start()
        bias_qkv += jnp.sum(dmixed.astype(F32), axis=0, keepdims=True)
        sum_s[0:1, :] += jnp.sum(dh1 * xh, axis=0, keepdims=True)
        sum_s[1:2, :] += jnp.sum(dh1, axis=0, keepdims=True)
        sum_s[2:3, :] += jnp.sum(dh2 * xh, axis=0, keepdims=True)
        sum_s[3:4, :] += jnp.sum(dh2, axis=0, keepdims=True)
    sum_s[4:5, :] = jnp.sum(dy[0:256, :].astype(F32), axis=0, keepdims=True)
    sum_s[5:6, :] = sums[0:1, :]
    for third, place in enumerate(bias_places(me)):
        sum_s[6 + third : 7 + third, :] = dot(bias_qkv.astype(BF), place)
    columns = sum_s[...].T[:, 0:64]
    for at in range(0, 768, 256):
        chunk = dot(h1_s[:, at : at + 256], dm_s[...], 0, 0)
        grads[at : at + 256, 256:896] = jnp.concatenate([chunk, columns[at : at + 256]], -1).astype(BF)
    for store in stores:
        store.wait()


def join_kernel(seq, grads, out_0, out_1, out_2, out_3, joined):
    for at, piece in enumerate((out_0, out_1, out_2, out_3)):
        joined[pl.ds(pl.multiple_of((seq[0] ^ at) * 192, 192), 192), :] = piece[...]


def place_kernel(every, up, down, qkv, out, *small):
    row = sublane(384)
    group = jnp.floor((row.astype(F32) + 0.5) * (1.0 / 96.0)).astype(jnp.int32)
    inner = row - 96 * group
    pick = one_hot(inner + 72 * by24(inner) + 24 * group, lane(384))
    parts = [every[at].astype(F32) for at in range(4)]
    for at in range(8):
        columns = jnp.concatenate([p[:, 96 * at : 96 * at + 96] for p in parts], -1).astype(BF)
        up[:, 384 * at : 384 * at + 384] = dot(columns, pick)
    down[...] = jnp.concatenate([p[:, 768:1536] for p in parts], 0)
    for kind in range(3):
        qkv[:, 768 * kind : 768 * kind + 768] = jnp.concatenate(
            [p[:, 1792 + 192 * kind : 1984 + 192 * kind] for p in parts], -1
        )
    out[...] = jnp.concatenate([p[:, 1536:1728] for p in parts], -1)
    pad = jnp.zeros((104, 64), F32)
    rows = [jnp.concatenate([p[:, 2368:2432], pad], 0).T for p in parts]
    total = rows[0] + rows[1] + rows[2] + rows[3]
    for at, ref in zip((0, 1, 2, 3, 4, 4), small):
        ref[...] = total[at, 0:24]
    small[6][...] = jnp.concatenate([total[at : at + 1, 0:24] for at in (6, 7, 8)], -1)[0]
    small[7][...] = jnp.concatenate([r[5:6, 0:24] for r in rows], -1)[0]


def whole(shape):
    return pl.BlockSpec(shape, lambda i: (0,) * len(shape))


def call(kernel, name, args, specs, outs, scratch=(), far=()):
    shapes = [jax.ShapeDtypeStruct(shape, dtype) for shape, dtype in outs]
    return pl.pallas_call(
        kernel,
        name=name,
        grid=(1,),
        in_specs=[whole(a.shape) if spec is None else spec for a, spec in zip(args, specs)],
        out_specs=[
            pl.BlockSpec(memory_space=pl.ANY) if at in far else whole(shape.shape) for at, shape in enumerate(shapes)
        ],
        out_shape=shapes,
        scratch_shapes=[pltpu.VMEM(*s) if isinstance(s, tuple) else s for s in scratch],
        cost_estimate=pl.CostEstimate(flops=1_000_000, bytes_accessed=100_000, transcendentals=0),
        compiler_params=pltpu.CompilerParams(vmem_limit_bytes=60 * 2**20),
    )(*args)


def per_device(x, dy, g1, b1, g2, b2, wqkv, bqkv, wo, bo, wu, bu, wd, bd):
    s = lax.axis_index("seq")
    d = lax.axis_index("dp").astype(jnp.int32)
    me = s.astype(jnp.int32).reshape(1)
    place = jnp.stack([s.astype(jnp.int32), d // 8, d // 2 % 4])
    scalar, far = pl.BlockSpec(memory_space=pltpu.SMEM), pl.BlockSpec(memory_space=pl.ANY)
    x, dy = x[0], dy[0]
    (packed,) = call(
        pack_kernel,
        "pack",
        (me, wqkv, wo, wu, wd, g1, b1, g2, b2, bo, bd, bu, bqkv),
        (scalar, *[None] * 12),
        [((24, 2944), BF)],
    )
    position = jnp.concatenate([(s ^ k) * 256 + jnp.arange(256, dtype=jnp.int32) for k in range(4)])
    tables = rotary_tables(position)
    other, both, *tables = lax.optimization_barrier((across_pair(packed), jnp.concatenate([x, dy]), *tables))
    left, right = dp_gather(packed, other, 1152)

    blocks = seq_gather(both, right[1:])

    wide, tall, lines = (1024, 768), ((1024, 768), BF), ((16, 768), F32)
    act, grads, sums, dup, w_v, w_out, vectors, xs, dys, w_d = call(
        mlp_kernel,
        "mlp",
        (place, x, dy, *blocks, left, *right),
        (scalar, *[far] * 5, whole((768, 768)), *[None] * 4),
        [(wide, BF), ((768, 1536), BF), ((8, 768), F32), (wide, BF), ((768, 192), BF), ((192, 768), BF), lines, (wide, BF), (wide, BF), ((768, 768), BF)],
        [
            *[tall] * 3,
            ((768, 768), BF),
            ((768, 128), F32),
            *[tall] * 2,
            pltpu.SemaphoreType.DMA((13,)),
        ],
        (0, 3, 7, 8, 9),
    )
    plane_first = plane_exchange(grads)
    weight, small, table = ((768, 768), BF), ((768, 192), BF), ((1024, 128), F32)
    mixed = ((1024, 576), BF)
    qkv, lse, *pieces = call(
        forward_kernel,
        "attention_forward",
        (me, vectors, left, w_v, xs, *tables, w_d, act, w_out, dys),
        (scalar, None, *[far] * 10),
        [mixed, ((8, 1024), F32), *[((192, 256), BF)] * 4, *[((2, 256, 768), BF)] * 2],
        [
            ((768, 1152), BF),
            small,
            tall,
            *[table] * 3,
            weight,
            tall,
            ((192, 768), BF),
            tall,
            mixed,
            ((4, 256, 768), BF),
            ((192, 256), F32),
            ((1024, 192), BF),
            ((4, 192, 192), BF),
            pltpu.SemaphoreType.DMA((15,)),
        ],
        (0, 6, 7),
    )
    g_out, part = pieces[:4], pieces[4:]
    g_out = [g_out[0]] + [swap(g_out[k], k) for k in range(1, 4)]

    grads, dx_kept, dx_sent = call(
        backward_kernel,
        "attention_backward",
        (me, dys, vectors, w_out, qkv, lse, sums, *tables, left, w_v, xs, dup),
        (scalar, *[None] * 6, *[far] * 7),
        [((768, 896), BF), ((2, 256, 768), BF), ((2, 256, 768), BF)],
        [
            *[table] * 3,
            ((768, 1152), BF),
            small,
            tall,
            tall,
            ((4, 256, 768), BF),
            ((1024, 192), BF),
            ((192, 1024), F32),
            ((1024, 192), F32),
            ((1024, 192), F32),
            mixed,
            ((128, 768), F32),
            tall,
            pltpu.SemaphoreType.DMA((11,)),
        ],
        (1, 2),
    )
    grads = pl.pallas_call(
        join_kernel,
        name="join",
        grid=(1,),
        in_specs=[scalar, far, *[whole((192, 256))] * 4],
        out_specs=pl.BlockSpec((768, 256), lambda i: (0, 0)),
        out_shape=jax.ShapeDtypeStruct((768, 896), BF),
        input_output_aliases={1: 0},
        cost_estimate=pl.CostEstimate(flops=1_000_000, bytes_accessed=100_000, transcendentals=0),
    )(me, grads, *g_out)
    grads, plane_first, dx_kept, dx_sent, *part = lax.optimization_barrier(
        (grads, plane_first, dx_kept, dx_sent, *part)
    )
    plane_second = plane_exchange(grads)
    block_output = (x.astype(F32) + seq_sum(*part)).astype(BF)
    dx_core, plane_first = lax.optimization_barrier((swap(dx_sent, 1), plane_first))
    dxhat = seq_rest(dx_kept, dx_core)
    xhat, rstd = normalize(x.astype(F32))
    dxhat = dxhat - jnp.mean(dxhat, axis=-1, keepdims=True) - xhat * jnp.mean(dxhat * xhat, axis=-1, keepdims=True)
    input_grad = (dy.astype(F32) + rstd * dxhat).astype(BF)
    sum_first, plane_second = lax.optimization_barrier((plane_sum(plane_first), plane_second))
    sums = jnp.concatenate([sum_first, plane_sum(plane_second)], axis=1)
    every = lax.all_gather(pair_sum(sums), "seq", axis=0)
    t_up, t_down, t_qkv, t_out, g_g1, g_b1, g_g2, g_b2, g_bo, g_bd, g_qkvb, g_upb = call(
        place_kernel,
        "place",
        (every,),
        (None,),
        [
            ((24, 3072), F32),
            ((96, 768), F32),
            ((24, 2304), F32),
            ((24, 768), F32),
            *[((24,), F32)] * 6,
            ((72,), F32),
            ((96,), F32),
        ],
    )
    return (
        block_output[None],
        input_grad[None],
        g_g1,
        g_b1,
        g_g2,
        g_b2,
        t_qkv,
        g_qkvb,
        t_out,
        g_bo,
        t_up,
        g_upb,
        t_down,
        g_bd,
    )


def solution(mesh):
    rows, vector, weight = P("dp", "seq", None), P("dp"), P("dp", None)
    params = (vector, vector, vector, vector, weight, vector, weight, vector, weight, vector, weight, vector)
    return jax.shard_map(
        per_device,
        mesh=mesh,
        in_specs=(rows, rows, *params),
        out_specs=(rows, rows, *params),
        check_vma=False,
    )
```

```python
import jax
import jax.numpy as jnp
from jax import lax
from jax.experimental import pallas as pl
from jax.experimental.pallas import tpu as pltpu
from jax.sharding import PartitionSpec as P

HD = 64
ROT = 16
F32 = jnp.float32
BF = jnp.bfloat16


def swap(value, bits):
    return lax.ppermute(value, "seq", [(s, s ^ bits) for s in range(4)])


def seq_gather(value, earlier):
    far = swap(value, 2)
    sent, *_ = lax.optimization_barrier((far, *earlier))
    return [swap(value, 1), far, swap(sent, 1)]


def seq_sum(kept, sent):
    return seq_rest(kept, swap(sent, 1))


def seq_rest(kept, core):
    core = core.astype(F32)
    far = (kept[1].astype(F32) + core[1]).astype(BF)
    return kept[0].astype(F32) + core[0] + swap(far, 2).astype(F32)


def dp_groups():
    return [[2 * p + z for p in range(16)] for z in range(2)]


def plane_exchange(parts):
    return lax.all_to_all(
        parts.reshape(16, 48, -1), "dp", split_axis=0, concat_axis=0, tiled=True, axis_index_groups=dp_groups()
    )


def dp_shift(value, along_y, along_x):
    pairs = []
    for d in range(32):
        y, x, z = d // 8, d // 2 % 4, d % 2
        pairs.append((d, ((y + along_y) % 4 * 4 + (x + along_x) % 4) * 2 + z))
    return lax.ppermute(value, "dp", pairs)


def across_pair(value):
    return lax.ppermute(value, "dp", [(d, d ^ 1) for d in range(32)])


SOURCES = (0, -1, 1, 2)


def line_gather(value, along):
    lines = [[2 * p + z for p in range(16) if (p // 4, p % 4)[along == "y"] == fixed] for fixed in range(4) for z in range(2)]
    copies = jnp.broadcast_to(value[None], (4, *value.shape))
    got = lax.all_to_all(copies, "dp", split_axis=0, concat_axis=0, tiled=True, axis_index_groups=lines)
    return got.reshape(4 * value.shape[0], -1)


def dp_gather(shard, other, cut, place):
    low = lax.axis_index("dp") % 2 == 0
    pair = jnp.concatenate([jnp.where(low, shard, other), jnp.where(low, other, shard)], axis=0)
    left, right = [pair[:, :cut]], [pair[:, cut:]]
    for step in (1, 2, 3):
        left.append(dp_shift(left[0], 0, -step))
        right.append(dp_shift(right[0], -SOURCES[step], 0))
    x = lax.axis_index("dp") // 2 % 4
    left = jnp.concatenate(
        [
            jnp.where(
                x < 2,
                jnp.where(x == 0, left[c], left[(c + 3) % 4]),
                jnp.where(x == 2, left[(c + 2) % 4], left[(c + 1) % 4]),
            )
            for c in range(4)
        ]
    )
    (first,) = call(
        half_kernel,
        "half",
        (place, *right),
        (pl.BlockSpec(memory_space=pltpu.SMEM), *[None] * 4),
        [((192, 1216), BF)],
    )
    right = [first]
    for step in SOURCES[1:]:
        right.append(dp_shift(right[0], 0, -step))
    return line_gather(left, "y"), right


def plane_sum(parts):
    return jnp.sum(parts.astype(F32), axis=0)


def pair_sum(total):
    half = lax.axis_index("dp") % 2
    kept = lax.dynamic_slice_in_dim(total, half * 24, 24, 0)
    sent = lax.dynamic_slice_in_dim(total, (1 - half) * 24, 24, 0).astype(BF)
    return (kept + across_pair(sent).astype(F32)).astype(BF)


def normalize(x):
    average = jnp.mean(x, axis=-1, keepdims=True)
    centered = x - average
    spread = jnp.mean(centered * centered, axis=-1, keepdims=True)
    rstd = lax.rsqrt(spread + 1e-05)
    return centered * rstd, rstd


def dot(a, b, ca=1, cb=0):
    return lax.dot_general(a, b, (((ca,), (cb,)), ((), ())), preferred_element_type=F32)


def rotary_tables(position):
    at = jnp.arange(2 * HD) % HD
    frequency = 10000.0 ** (-2.0 * (at % (ROT // 2)).astype(F32) / ROT)
    angles = position.astype(F32)[:, None] * frequency[None, :]
    own = jnp.where(at < ROT, jnp.cos(angles), 1.0)
    sine = jnp.sin(angles)
    above = jnp.where(at < ROT // 2, -sine, 0.0)
    below = jnp.where((at >= ROT // 2) & (at < ROT), sine, 0.0)
    return own, above, below


def turn(block, own, above, below):
    columns = []
    for at in range(0, 384, 128):
        part = block[:, at : at + 128]
        columns.append(part * own + pltpu.roll(part, 120, 1) * above + pltpu.roll(part, 8, 1) * below)
    return jnp.concatenate(columns, -1)


def causal(shape):
    return lax.broadcasted_iota(jnp.int32, shape, 0) <= lax.broadcasted_iota(jnp.int32, shape, 1)


def by24(index):
    return jnp.floor((index.astype(F32) + 0.5) * (1.0 / 24.0)).astype(jnp.int32)


def lane(n):
    return lax.broadcasted_iota(jnp.int32, (1, n), 1)


def sublane(n):
    return lax.broadcasted_iota(jnp.int32, (n, 1), 0)


def one_hot(rows, columns):
    return jnp.where(rows == columns, 1.0, 0.0).astype(BF)


def bias_places(me):
    column = sublane(576)
    column = column + 576 * ((column >= 192).astype(jnp.int32) + (column >= 384).astype(jnp.int32)) + 192 * me
    target = lane(768)
    target = target + 48 * by24(target)
    return [one_hot(column, target + 24 * third) for third in range(3)]


def pack_kernel(seq, wqkv, wo, wu, wd, g1, b1, g2, b2, bo, bd, bu, bqkv, out):
    me = seq[0]

    def chosen(pieces):
        result = pieces[0]
        for at in range(1, 4):
            result = jnp.where(me == at, pieces[at], result)
        return result

    target = lane(384)
    target = target + 72 * by24(target) + 24 * me
    pick = one_hot(sublane(1536), target)
    up = [dot(wu[:, 0:1536], pick), dot(wu[:, 1536:3072], pick)]
    rows = wd[...].astype(F32)
    down = chosen([rows[24 * q : 24 * q + 24] for q in range(4)])
    columns = wqkv[...].astype(F32)
    qkv = [chosen([columns[:, k + 192 * q : k + 192 * q + 192] for q in range(4)]) for k in (0, 768, 1536)]
    outs = wo[...].astype(F32)
    rows = [ref[...].astype(F32).reshape(1, 24) for ref in (g1, b1, g2, b2, bo, bd)]
    bias = bu[...].astype(F32).reshape(1, 96)
    rows.append(chosen([bias[:, 24 * q : 24 * q + 24] for q in range(4)]))
    bias = bqkv[...].astype(F32).reshape(1, 72)
    rows += [bias[:, 24 * q : 24 * q + 24] for q in range(3)]
    vectors = jnp.concatenate(rows + [jnp.zeros((6, 24), F32)], axis=0)
    vectors = jnp.concatenate([vectors, jnp.zeros((16, 104), F32)], axis=1)
    vectors = jnp.concatenate([vectors, jnp.zeros((112, 128), F32)], axis=0).T[0:24, 0:64]
    out[...] = jnp.concatenate([*up, *qkv[:2], down, qkv[2], vectors, outs], axis=1).astype(BF)


def normal(rows):
    rows = rows.astype(F32)
    centered = rows - jnp.mean(rows, axis=-1, keepdims=True)
    spread = jnp.mean(centered * centered, axis=-1, keepdims=True)
    return centered * lax.rsqrt(spread + 1e-05)


def rows_of(place, outer, inner):
    one = lax.rem(place[1] + (SOURCES[inner] + 4), 4) * 4 + lax.rem(place[2] + (SOURCES[outer] + 4), 4)
    return pl.ds(pl.multiple_of(one * 48, 48), 48)


def half_kernel(place, right_0, right_1, right_2, right_3, out):
    for at, right in enumerate((right_0, right_1, right_2, right_3)):
        out[48 * at : 48 * at + 48, 0:1024] = right[:, 0:1024]

        @pl.when(lax.rem(place[1] + (SOURCES[at] + 4), 4) == place[0])
        def _():
            for column in range(4):
                out[48 * column : 48 * column + 48, 1024:1216] = right[:, 1024 + 192 * column : 1216 + 192 * column]


def mlp_kernel(
    place, x_own, dy_own, core, opposite, across, wu, right_0, right_1, right_2, right_3,
    act_far, grads_far, sums, dup_far, wv, wo, vectors, xs_far, dy_far, wd_far,
    h2_s, act_s, dup_s, wd, vec_s, xs, dy, grads, moved,
):
    own = [(x_own, xs, 0, 0), (dy_own, dy, 0, 0)]
    for at, ref in enumerate((core, opposite, across)):
        own += [(ref, xs, 0, at + 1), (ref, dy, 256, at + 1)]
    loads = [
        pltpu.make_async_copy(ref.at[first : first + 256], to.at[256 * at : 256 * at + 256], moved.at[k])
        for k, (ref, to, first, at) in enumerate(own)
    ]
    for load in loads:
        load.start()
    for outer, right in enumerate((right_0, right_1, right_2, right_3)):
        for inner in range(4):
            rows = rows_of(place, outer, inner)
            piece = right[inner * 48 : inner * 48 + 48, :]
            wd[rows, :] = piece[:, 0:768]
            wv[rows, :] = piece[:, 768:960]
            vec_s[rows, 0:64] = piece[:, 960:1024].astype(F32)
            rows = pl.ds(pl.multiple_of(lax.rem(place[2] + (SOURCES[outer] + 4), 4) * 48, 48), 48)
            wo[rows, 192 * inner : 192 * inner + 192] = piece[:, 1024:1216]
    vectors[...] = vec_s[...].T[0:16]
    for load in loads:
        load.wait()
    stores = [
        pltpu.make_async_copy(ref, to, moved.at[8 + k])
        for k, (ref, to) in enumerate(((xs, xs_far), (dy, dy_far), (wd, wd_far), (act_s, act_far), (dup_s, dup_far)))
    ]
    for store in stores[:3]:
        store.start()
    sums[...] = jnp.zeros_like(sums)

    @pl.loop(0, 4, unroll=4)
    def _(step):
        rows = pl.ds(pl.multiple_of(step * 256, 256), 256)
        xh = normal(xs[rows, :])
        gain = vectors[2:3, :]
        h2 = (xh * gain + vectors[3:4, :]).astype(BF)
        h2_s[rows, :] = h2
        upper = dot(h2, wu[...]) + vectors[6:7, :]
        phi = 0.5 + 0.5 * lax.erf(upper * 0.7071067811865476)
        active = (upper * phi).astype(BF)
        act_s[rows, :] = active
        slope = phi + upper * (jnp.exp(-0.5 * upper * upper) * 0.3989422804014327)
        dup = (dot(dy[rows, :], wd[...], 1, 1) * slope).astype(BF)
        dup_s[rows, :] = dup
        sums[0:1, :] += jnp.sum(dup.astype(F32), axis=0, keepdims=True)

    stores[3].start()
    stores[4].start()
    for at in range(0, 768, 256):
        grads[at : at + 256, 0:768] = dot(h2_s[:, at : at + 256], dup_s[...], 0, 0).astype(BF)
        grads[at : at + 256, 768:1536] = dot(act_s[:, at : at + 256], dy[...], 0, 0).astype(BF)
        stores.append(
            pltpu.make_async_copy(
                grads.at[at : at + 256], grads_far.at[at : at + 256], moved.at[13 + at // 256]
            )
        )
        stores[-1].start()
    for store in stores:
        store.wait()


def forward_kernel(
    seq, vec_s, *refs
):
    me = seq[0]
    far, (qkv_far, lse, out_0, out_1, out_2, out_3, part_kept, part_sent) = refs[:10], refs[10:18]
    near, (qkv, part, ctx_s, total, pieces, moved) = refs[18:28], refs[28:]
    loads = [pltpu.make_async_copy(far[k], near[k], moved.at[k]) for k in range(10)]
    for load in loads:
        load.start()
    wqk, wv, xs, own, above, below, wd, act, wo, dy = near
    bias_out = jnp.where(me == 0, vec_s[4:5, :] + vec_s[5:6, :], 0.0)
    bias_qkv = jnp.zeros((1, 576), F32)
    for third, place in enumerate(bias_places(me)):
        bias_qkv += dot(vec_s[7 + third : 8 + third, :].astype(BF), place, 1, 1)

    for load in loads[:6]:
        load.wait()

    @pl.loop(0, 4, unroll=2)
    def _(step):
        rows = pl.ds(pl.multiple_of(step * 256, 256), 256)
        place = pl.ds(pl.multiple_of((step ^ me) * 256, 256), 256)
        h = (normal(xs[rows, :]) * vec_s[0:1, :] + vec_s[1:2, :]).astype(BF)
        mixed = dot(h, wqk[:, 768:1152]) + bias_qkv[:, 0:384]
        qkv[place, 0:384] = turn(mixed, own[rows, :], above[rows, :], below[rows, :]).astype(BF)
        qkv[place, 384:576] = (dot(h, wv[...]) + bias_qkv[:, 384:576]).astype(BF)

    store = pltpu.make_async_copy(qkv, qkv_far, moved.at[10])
    store.start()
    for load in loads[6:]:
        load.wait()
    allowed = causal((256, 256))
    for block in range(4):
        first, keys = block * 256, block * 256 + 256
        for head in range(3):
            at = head * 64
            query = qkv[first:keys, at : at + 64] * 0.125
            scores = dot(qkv[0:keys, 192 + at : 256 + at], query, 1, 1)
            last = jnp.where(allowed, scores[first:], -1e30)
            scores = jnp.concatenate([scores[:first], last], 0) if block else last
            top = jnp.max(scores, axis=0, keepdims=True)
            weight = jnp.exp(scores - top)
            count = jnp.sum(weight, axis=0, keepdims=True)
            lse[head : head + 1, first:keys] = top + jnp.log(count)
            context = dot(qkv[0:keys, 384 + at : 448 + at], weight.astype(BF), 0, 0)
            ctx_s[at : at + 64, :] = context / count
        place = pl.ds(pl.multiple_of((me ^ block) * 256, 256), 256)
        context = ctx_s[...].T.astype(BF)
        total[place, :] = context
        part[me ^ block] = (dot(act[place, :], wd[...]) + dot(context, wo[...]) + bias_out).astype(BF)
    stores = [store]
    for at in range(4):
        to = (part_sent if at % 2 else part_kept).at[at // 2]
        stores.append(pltpu.make_async_copy(part.at[at], to, moved.at[11 + at]))
        stores[-1].start()
    rows = dot(total[...], dy[...], 0, 0)
    for column in range(4):
        pieces[column] = rows[:, 192 * column : 192 * column + 192].astype(BF)
    for at, ref in enumerate((out_0, out_1, out_2, out_3)):
        ref[:, 0:192] = pieces[at ^ me]
        ref[:, 192:256] = jnp.zeros((192, 64), BF)
    for store in stores:
        store.wait()


def backward_kernel(
    seq, dy, vec_s, wo, qkv, lse, sums, *refs
):
    me = seq[0]
    far, (grads, kept_far, sent_far) = refs[:7], refs[7:10]
    near, (dx, do_s, dq_s, dk_s, dv_s, dm_s, sum_s, h1_s, moved) = refs[10:17], refs[17:]
    loads = [pltpu.make_async_copy(far[k], near[k], moved.at[k]) for k in range(7)]
    for load in loads:
        load.start()
    own, above, below, left, wv, xs, dup = near
    sum_s[...] = jnp.zeros_like(sum_s)

    @pl.loop(0, 4)
    def _(step):
        rows = pl.ds(pl.multiple_of(step * 256, 256), 256)
        place = pl.ds(pl.multiple_of((step ^ me) * 256, 256), 256)
        do_s[place, :] = dot(dy[rows, :], wo[...], 1, 1).astype(BF)

    allowed = causal((512, 512))
    for block in reversed(range(2)):
        first, keys = block * 512, block * 512 + 512
        for head in range(3):
            at = head * 64
            query = qkv[first:keys, at : at + 64] * 0.125
            key = qkv[0:keys, 192 + at : 256 + at]
            dcontext = do_s[first:keys, at : at + 64]
            scores = dot(key, query, 1, 1)
            last = jnp.where(allowed, scores[first:], -1e30)
            scores = jnp.concatenate([scores[:first], last], 0) if block else last
            probs = jnp.exp(scores - lse[head : head + 1, first:keys])
            dprobs = dot(qkv[0:keys, 384 + at : 448 + at], dcontext, 1, 1)
            delta = jnp.sum(probs * dprobs, axis=0, keepdims=True)
            dscores = (probs * (dprobs - delta)).astype(BF)
            dv = dot(probs.astype(BF), dcontext)
            dk = dot(dscores, query)
            if block == 1:
                dv_s[:, at : at + 64] = dv
                dk_s[:, at : at + 64] = dk
            else:
                dv_s[0:keys, at : at + 64] += dv
                dk_s[0:keys, at : at + 64] += dk
            dq_s[at : at + 64, first:keys] = dot(key, dscores, 0, 0) * 0.125

    for load in loads:
        load.wait()
    for block in range(4):
        first, keys = block * 256, block * 256 + 256
        place = pl.ds(pl.multiple_of((me ^ block) * 256, 256), 256)
        both = jnp.concatenate([dq_s[:, first:keys].T, dk_s[first:keys, :]], -1)
        both = both.astype(BF).astype(F32)
        both = turn(both, own[place, :], -above[place, :], -below[place, :])
        dm_s[place, 0:384] = both.astype(BF)
        dm_s[place, 384:576] = dv_s[first:keys, :].astype(BF)

    stores = []
    bias_qkv = jnp.zeros((1, 576), F32)
    for step in range(4):
        rows = slice(step * 256, step * 256 + 256)
        dmixed = dm_s[rows, :]
        xh = normal(xs[rows, :])
        h1_s[rows, :] = (xh * vec_s[0:1, :] + vec_s[1:2, :]).astype(BF)
        dh1 = dot(dmixed[:, 0:384], left[:, 768:1152], 1, 1) + dot(dmixed[:, 384:576], wv[...], 1, 1)
        dh2 = dot(dup[rows, :], left[:, 0:768], 1, 1)
        dx[step] = (dh1 * vec_s[0:1, :] + dh2 * vec_s[2:3, :]).astype(BF)
        to = (sent_far if step % 2 else kept_far).at[step // 2]
        stores.append(pltpu.make_async_copy(dx.at[step], to, moved.at[7 + step]))
        stores[-1].start()
        bias_qkv += jnp.sum(dmixed.astype(F32), axis=0, keepdims=True)
        sum_s[0:1, :] += jnp.sum(dh1 * xh, axis=0, keepdims=True)
        sum_s[1:2, :] += jnp.sum(dh1, axis=0, keepdims=True)
        sum_s[2:3, :] += jnp.sum(dh2 * xh, axis=0, keepdims=True)
        sum_s[3:4, :] += jnp.sum(dh2, axis=0, keepdims=True)
    sum_s[4:5, :] = jnp.sum(dy[0:256, :].astype(F32), axis=0, keepdims=True)
    sum_s[5:6, :] = sums[0:1, :]
    for third, place in enumerate(bias_places(me)):
        sum_s[6 + third : 7 + third, :] = dot(bias_qkv.astype(BF), place)
    columns = sum_s[...].T[:, 0:64]
    for at in range(0, 768, 256):
        chunk = dot(h1_s[:, at : at + 256], dm_s[...], 0, 0)
        grads[at : at + 256, 256:896] = jnp.concatenate([chunk, columns[at : at + 256]], -1).astype(BF)
    for store in stores:
        store.wait()


def join_kernel(seq, grads, out_0, out_1, out_2, out_3, joined):
    for at, piece in enumerate((out_0, out_1, out_2, out_3)):
        joined[pl.ds(pl.multiple_of((seq[0] ^ at) * 192, 192), 192), :] = piece[...]


def place_kernel(every, up, down, qkv, out, *small):
    row = sublane(384)
    group = jnp.floor((row.astype(F32) + 0.5) * (1.0 / 96.0)).astype(jnp.int32)
    inner = row - 96 * group
    pick = one_hot(inner + 72 * by24(inner) + 24 * group, lane(384))
    parts = [every[at].astype(F32) for at in range(4)]
    for at in range(8):
        columns = jnp.concatenate([p[:, 96 * at : 96 * at + 96] for p in parts], -1).astype(BF)
        up[:, 384 * at : 384 * at + 384] = dot(columns, pick)
    down[...] = jnp.concatenate([p[:, 768:1536] for p in parts], 0)
    for kind in range(3):
        qkv[:, 768 * kind : 768 * kind + 768] = jnp.concatenate(
            [p[:, 1792 + 192 * kind : 1984 + 192 * kind] for p in parts], -1
        )
    out[...] = jnp.concatenate([p[:, 1536:1728] for p in parts], -1)
    pad = jnp.zeros((104, 64), F32)
    rows = [jnp.concatenate([p[:, 2368:2432], pad], 0).T for p in parts]
    total = rows[0] + rows[1] + rows[2] + rows[3]
    for at, ref in zip((0, 1, 2, 3, 4, 4), small):
        ref[...] = total[at, 0:24]
    small[6][...] = jnp.concatenate([total[at : at + 1, 0:24] for at in (6, 7, 8)], -1)[0]
    small[7][...] = jnp.concatenate([r[5:6, 0:24] for r in rows], -1)[0]


def whole(shape):
    return pl.BlockSpec(shape, lambda i: (0,) * len(shape))


def call(kernel, name, args, specs, outs, scratch=(), far=()):
    shapes = [jax.ShapeDtypeStruct(shape, dtype) for shape, dtype in outs]
    return pl.pallas_call(
        kernel,
        name=name,
        grid=(1,),
        in_specs=[whole(a.shape) if spec is None else spec for a, spec in zip(args, specs)],
        out_specs=[
            pl.BlockSpec(memory_space=pl.ANY) if at in far else whole(shape.shape) for at, shape in enumerate(shapes)
        ],
        out_shape=shapes,
        scratch_shapes=[pltpu.VMEM(*s) if isinstance(s, tuple) else s for s in scratch],
        cost_estimate=pl.CostEstimate(flops=1_000_000, bytes_accessed=100_000, transcendentals=0),
        compiler_params=pltpu.CompilerParams(vmem_limit_bytes=60 * 2**20),
    )(*args)


def per_device(x, dy, g1, b1, g2, b2, wqkv, bqkv, wo, bo, wu, bu, wd, bd):
    s = lax.axis_index("seq")
    d = lax.axis_index("dp").astype(jnp.int32)
    me = s.astype(jnp.int32).reshape(1)
    place = jnp.stack([s.astype(jnp.int32), d // 8, d // 2 % 4])
    scalar, far = pl.BlockSpec(memory_space=pltpu.SMEM), pl.BlockSpec(memory_space=pl.ANY)
    x, dy = x[0], dy[0]
    (packed,) = call(
        pack_kernel,
        "pack",
        (me, wqkv, wo, wu, wd, g1, b1, g2, b2, bo, bd, bu, bqkv),
        (scalar, *[None] * 12),
        [((24, 2944), BF)],
    )
    position = jnp.concatenate([(s ^ k) * 256 + jnp.arange(256, dtype=jnp.int32) for k in range(4)])
    tables = rotary_tables(position)
    other, both, *tables = lax.optimization_barrier((across_pair(packed), jnp.concatenate([x, dy]), *tables))
    left, right = dp_gather(packed, other, 1152, place)

    blocks = seq_gather(both, right[1:])

    wide, tall, lines = (1024, 768), ((1024, 768), BF), ((16, 768), F32)
    act, grads, sums, dup, w_v, w_out, vectors, xs, dys, w_d = call(
        mlp_kernel,
        "mlp",
        (place, x, dy, *blocks, left, *right),
        (scalar, *[far] * 5, whole((768, 768)), *[None] * 4),
        [(wide, BF), ((768, 1536), BF), ((8, 768), F32), (wide, BF), ((768, 192), BF), ((192, 768), BF), lines, (wide, BF), (wide, BF), ((768, 768), BF)],
        [
            *[tall] * 3,
            ((768, 768), BF),
            ((768, 128), F32),
            *[tall] * 2,
            ((768, 1536), BF),
            pltpu.SemaphoreType.DMA((16,)),
        ],
        (0, 1, 3, 7, 8, 9),
    )
    plane_first = plane_exchange(grads)
    weight, small, table = ((768, 768), BF), ((768, 192), BF), ((1024, 128), F32)
    mixed = ((1024, 576), BF)
    qkv, lse, *pieces = call(
        forward_kernel,
        "attention_forward",
        (me, vectors, left, w_v, xs, *tables, w_d, act, w_out, dys),
        (scalar, None, *[far] * 10),
        [mixed, ((8, 1024), F32), *[((192, 256), BF)] * 4, *[((2, 256, 768), BF)] * 2],
        [
            ((768, 1152), BF),
            small,
            tall,
            *[table] * 3,
            weight,
            tall,
            ((192, 768), BF),
            tall,
            mixed,
            ((4, 256, 768), BF),
            ((192, 256), F32),
            ((1024, 192), BF),
            ((4, 192, 192), BF),
            pltpu.SemaphoreType.DMA((15,)),
        ],
        (0, 6, 7),
    )
    g_out, part = pieces[:4], pieces[4:]
    g_out = [g_out[0]] + [swap(g_out[k], k) for k in range(1, 4)]

    grads, dx_kept, dx_sent = call(
        backward_kernel,
        "attention_backward",
        (me, dys, vectors, w_out, qkv, lse, sums, *tables, left, w_v, xs, dup),
        (scalar, *[None] * 6, *[far] * 7),
        [((768, 896), BF), ((2, 256, 768), BF), ((2, 256, 768), BF)],
        [
            *[table] * 3,
            ((768, 1152), BF),
            small,
            tall,
            tall,
            ((4, 256, 768), BF),
            ((1024, 192), BF),
            ((192, 1024), F32),
            ((1024, 192), F32),
            ((1024, 192), F32),
            mixed,
            ((128, 768), F32),
            tall,
            pltpu.SemaphoreType.DMA((11,)),
        ],
        (1, 2),
    )
    grads = pl.pallas_call(
        join_kernel,
        name="join",
        grid=(1,),
        in_specs=[scalar, far, *[whole((192, 256))] * 4],
        out_specs=pl.BlockSpec((768, 256), lambda i: (0, 0)),
        out_shape=jax.ShapeDtypeStruct((768, 896), BF),
        input_output_aliases={1: 0},
        cost_estimate=pl.CostEstimate(flops=1_000_000, bytes_accessed=100_000, transcendentals=0),
    )(me, grads, *g_out)
    grads, plane_first, dx_kept, dx_sent, *part = lax.optimization_barrier(
        (grads, plane_first, dx_kept, dx_sent, *part)
    )
    plane_second = plane_exchange(grads)
    block_output = (x.astype(F32) + seq_sum(*part)).astype(BF)
    dx_core, plane_first = lax.optimization_barrier((swap(dx_sent, 1), plane_first))
    dxhat = seq_rest(dx_kept, dx_core)
    xhat, rstd = normalize(x.astype(F32))
    dxhat = dxhat - jnp.mean(dxhat, axis=-1, keepdims=True) - xhat * jnp.mean(dxhat * xhat, axis=-1, keepdims=True)
    input_grad = (dy.astype(F32) + rstd * dxhat).astype(BF)
    sum_first, plane_second = lax.optimization_barrier((plane_sum(plane_first), plane_second))
    sums = jnp.concatenate([sum_first, plane_sum(plane_second)], axis=1)
    every = lax.all_gather(pair_sum(sums), "seq", axis=0)
    t_up, t_down, t_qkv, t_out, g_g1, g_b1, g_g2, g_b2, g_bo, g_bd, g_qkvb, g_upb = call(
        place_kernel,
        "place",
        (every,),
        (None,),
        [
            ((24, 3072), F32),
            ((96, 768), F32),
            ((24, 2304), F32),
            ((24, 768), F32),
            *[((24,), F32)] * 6,
            ((72,), F32),
            ((96,), F32),
        ],
    )
    return (
        block_output[None],
        input_grad[None],
        g_g1,
        g_b1,
        g_g2,
        g_b2,
        t_qkv,
        g_qkvb,
        t_out,
        g_bo,
        t_up,
        g_upb,
        t_down,
        g_bd,
    )


def solution(mesh):
    rows, vector, weight = P("dp", "seq", None), P("dp"), P("dp", None)
    params = (vector, vector, vector, vector, weight, vector, weight, vector, weight, vector, weight, vector)
    return jax.shard_map(
        per_device,
        mesh=mesh,
        in_specs=(rows, rows, *params),
        out_specs=(rows, rows, *params),
        check_vma=False,
    )
```
